32 devices in a mesh: space: 8 (over y, x, core), head: 4 (over z).
Axes of the slice: x: 2, y: 2, z: 4, core: 2. Of those that a mesh axis runs over, the one named last changes fastest.
Arguments:
- snapshot: bfloat16 [8192, 1536], P('space'), may hold values from -6 to 6
- norm_gain: float32 [1536], replicated, may hold values from 0.25 to 1.75
- w_query: bfloat16 [1536, 1536], P(None, 'head'), may hold values from -0.15625 to 0.15625
- w_key: bfloat16 [1536, 1536], P(None, 'head'), may hold values from -0.15625 to 0.15625
- w_value: bfloat16 [1536, 1536], P(None, 'head'), may hold values from -0.15625 to 0.15625
- w_out: bfloat16 [1536, 1536], P('head'), may hold values from -0.15625 to 0.15625
- cache_key: bfloat16 [8, 8192, 1536], P(None, 'space', 'head'), may hold values from -420 to 420
- cache_value: bfloat16 [8, 8192, 1536], P(None, 'space', 'head'), may hold values from -6 to 6
- pattern: int32 [64, 8], P('space'), may hold values from 0 to 63, as said below
- counts: int32 [64], P('space'), may hold values from 1 to 8, as said below
Outputs:
- rolled: bfloat16 [8192, 1536], P('space')
The draws below stay inside these ranges and needn't reach their ends.
Inputs may be any that keep to these rules, and one draw needn't show every extreme that they name: `pattern`: each index is a block within 12 blocks of its query block, counted periodically over the 64 blocks; the 8 entries of one query block are distinct. `counts`: loads are uneven; some query block has all 8 slots live.
All inputs are finite; a program needn't handle non-finite values.
Results may differ from the reference program's by a relative error of at most 0.014.
Values may be sent and summed in bfloat16 or wider, within the bound.
No kernel may reach another device: no remote copies, remote signals or barrier semaphores. Data moves between devices by JAX's collectives and lax.ppermute only.
A program may use at most 192 MiB of HBM per device.

```python
import jax
import jax.numpy as jnp
from jax import lax

HD = 128
H = 12
D = 1536
BLK = 128
MAXK = 8
FRAMES = 8
STEPS = 2
TOKENS = 8192
NBLK = 64
REACH = 12
N_HEAD = 4


def draw_pattern(key, part):
    row_keys = jax.random.split(key, NBLK)
    orders = jax.vmap(lambda row_key: jax.random.permutation(row_key, 2 * REACH + 1))(row_keys)
    offsets = orders[:, :MAXK].astype(jnp.int32) - REACH
    return ((jnp.arange(NBLK, dtype=jnp.int32)[:, None] + offsets) % NBLK).astype(jnp.int32)


def draw_counts(key, part):
    loads = jax.random.randint(key, (NBLK,), 1, MAXK + 1).astype(jnp.int32)
    picked = jax.random.randint(jax.random.fold_in(key, 7), (), 0, NBLK)
    return loads.at[picked].set(MAXK).astype(jnp.int32)


def draw_cache_key(key, part):
    values = jax.random.truncated_normal(key, -6.0, 6.0, (FRAMES, TOKENS, D), jnp.float32)
    return values.astype(jnp.bfloat16)


def steps_of(own_key, shape, pieces, low, top_value):
    def one(position, blocks):
        draws = jax.random.uniform(jax.random.fold_in(jax.random.fold_in(own_key, 6), position), (blocks,), jnp.float32, low / len(pieces), top_value / len(pieces))
        return jnp.repeat(jnp.exp(draws), shape[position] // blocks).reshape((-1,) + (1,) * (len(shape) - position - 1))

    loudness = one(*pieces[0])
    for cut in pieces[1:]:
        loudness = loudness * one(*cut)
    return loudness


def gaussian(key, shape, scale, reach, shards=(), kind=jnp.bfloat16):
    values = jax.random.normal(key, shape, jnp.float32) * scale
    if len(shards) > 0:
        values = steps_of(key, shape, shards, -0.22, 0.18) * values
    return jnp.clip(values, min=-reach, max=reach).astype(kind)


def setup_inputs(seed: int = 0) -> dict:
    arg_keys = jax.random.split(jax.random.key(seed), 11)
    return {
        "snapshot": gaussian(arg_keys[0], (TOKENS, D), 1.0, 6.0, ((0, 8),)),
        "norm_gain": jnp.clip(1.0 + 0.15 * jax.random.normal(arg_keys[1], (D,), jnp.float32), 0.25, 1.75),
        "w_query": gaussian(arg_keys[2], (D, D), D ** -0.5, 0.15625, ((1, 4),)),
        "w_key": gaussian(arg_keys[3], (D, D), D ** -0.5, 0.15625, ((1, 4),)),
        "w_value": gaussian(arg_keys[4], (D, D), D ** -0.5, 0.15625, ((1, 4),)),
        "w_out": gaussian(arg_keys[5], (D, D), D ** -0.5, 0.15625, ((0, 4),)),
        "cache_key": draw_cache_key(jax.random.fold_in(arg_keys[10], 71), 0),
        "cache_value": gaussian(arg_keys[7], (FRAMES, TOKENS, D), 1.0, 6.0, ((1, 8), (2, 4))),
        "pattern": draw_pattern(jax.random.fold_in(arg_keys[10], 71), 0),
        "counts": draw_counts(jax.random.fold_in(arg_keys[10], 71), 0),
    }


def attend_block(index, queries, key_complete, value_all, past_key, past_value, pattern, counts):
    inv_scale = 1.0 / HD ** 0.5
    block_query = lax.dynamic_slice_in_dim(queries, index * BLK, BLK, 0).astype(jnp.float32).reshape(BLK, H, HD)
    chosen = pattern[index]
    key_blocks = key_complete.reshape(NBLK, BLK, D)[chosen].astype(jnp.float32).reshape(MAXK, BLK, H, HD)
    value_blocks = value_all.reshape(NBLK, BLK, D)[chosen].astype(jnp.float32).reshape(MAXK, BLK, H, HD)
    cached_key = lax.dynamic_slice_in_dim(past_key, index * BLK, BLK, 1).astype(jnp.float32).reshape(FRAMES, BLK, H, HD)
    cached_value = lax.dynamic_slice_in_dim(past_value, index * BLK, BLK, 1).astype(jnp.float32).reshape(FRAMES, BLK, H, HD)
    spatial = jnp.einsum('qhd,jkhd->hqjk', block_query, key_blocks) * inv_scale
    live_slot = jnp.arange(MAXK) < counts[index]
    spatial = jnp.where(live_slot[None, None, :, None], spatial, jnp.float32(-1e+30))
    temporal = jnp.einsum('qhd,fqhd->hqf', block_query, cached_key) * inv_scale
    top_score = jnp.maximum(spatial.max(axis=(2, 3)), temporal.max(axis=2))
    spatial_exponent = jnp.exp(spatial - top_score[:, :, None, None])
    temporal_exp = jnp.exp(temporal - top_score[:, :, None])
    total = spatial_exponent.sum(axis=(2, 3)) + temporal_exp.sum(axis=2)
    spatial_attention_weight = (spatial_exponent / total[:, :, None, None]).astype(jnp.bfloat16).astype(jnp.float32)
    temporal_weight = (temporal_exp / total[:, :, None]).astype(jnp.bfloat16).astype(jnp.float32)
    mixed = jnp.einsum('hqjk,jkhd->qhd', spatial_attention_weight, value_blocks)
    mixed = mixed + jnp.einsum('hqf,fqhd->qhd', temporal_weight, cached_value)
    return mixed.reshape(BLK, D).astype(jnp.bfloat16)

def reference(snapshot, norm_gain, w_query, w_key, w_value, w_out, cache_key, cache_value, pattern, counts):
    state = snapshot
    past_key, past_value = (cache_key, cache_value)
    group_width = D // N_HEAD
    for rollout in range(STEPS):
        state_wide = state.astype(jnp.float32)
        meansq = lax.optimization_barrier(jnp.mean(state_wide * state_wide, axis=-1, keepdims=True))
        normed = (state_wide * lax.rsqrt(meansq + 1e-05) * norm_gain).astype(jnp.bfloat16)
        queries = jnp.dot(normed, w_query, preferred_element_type=jnp.float32).astype(jnp.bfloat16)
        key_new = jnp.dot(normed, w_key, preferred_element_type=jnp.float32).astype(jnp.bfloat16)
        value_new = jnp.dot(normed, w_value, preferred_element_type=jnp.float32).astype(jnp.bfloat16)
        attended_output = lax.map(lambda index: attend_block(index, queries, key_new, value_new, past_key, past_value, pattern, counts), jnp.arange(NBLK, dtype=jnp.int32))
        attended_output = attended_output.reshape(TOKENS, D)
        update = jnp.zeros((TOKENS, D), jnp.float32)
        for group in range(N_HEAD):
            partial_term = jnp.dot(attended_output[:, group * group_width:(group + 1) * group_width], w_out[group * group_width:(group + 1) * group_width], preferred_element_type=jnp.float32)
            rounded = lax.optimization_barrier(partial_term.astype(jnp.bfloat16))
            update = update + rounded.astype(jnp.float32)
        state = (state_wide + update).astype(jnp.bfloat16)
        if rollout + 1 < STEPS:
            past_key = jnp.concatenate([past_key[1:], key_new[None]], axis=0)
            past_value = jnp.concatenate([past_value[1:], value_new[None]], axis=0)
    return state
```

```python
import functools
import math

import jax
import jax.numpy as jnp
from jax import lax
from jax.experimental import pallas as pl
from jax.experimental.pallas import tpu as pltpu
from jax.sharding import PartitionSpec as P

HD = 128
BLK = 128
STEPS = 2
TILE = 256
VMEM_LIMIT = 48 * 1024 * 1024
NT = (((1,), (1,)), ((), ()))


def shifted(value, axis, steps):
    count = lax.axis_size(axis)
    pairs = [(source, (source + steps) % count) for source in range(count)]
    return lax.ppermute(value, axis, pairs)


def around(value, axis):
    count = lax.axis_size(axis)
    order = list(range(0, count, 2)) + list(range(1, count, 2))[::-1]
    pairs = [(order[i], order[(i + 1) % count]) for i in range(count)]
    return lax.ppermute(value, axis, pairs)


def call(body, grid, in_specs, out_specs, out_shape, scratch=(), prefetch=0, flops=0, moved=0, exps=0):
    return pl.pallas_call(
        body,
        grid_spec=pltpu.PrefetchScalarGridSpec(
            num_scalar_prefetch=prefetch,
            grid=grid,
            in_specs=in_specs,
            out_specs=out_specs,
            scratch_shapes=list(scratch),
        ),
        out_shape=out_shape,
        compiler_params=pltpu.CompilerParams(
            dimension_semantics=("arbitrary",) * len(grid), vmem_limit_bytes=VMEM_LIMIT
        ),
        cost_estimate=pl.CostEstimate(flops=flops, bytes_accessed=moved, transcendentals=exps),
    )


def dot(a, b):
    return jnp.dot(a, b, preferred_element_type=jnp.float32)


def normalize(state, gain):
    meansq = jnp.mean(state * state, axis=-1, keepdims=True)
    return (state * lax.rsqrt(meansq + 1e-05) * gain).astype(jnp.bfloat16)


def store_blocks(kv_ref, key, value):
    for block in range(key.shape[0] // BLK):
        rows = slice(block * BLK, (block + 1) * BLK)
        kv_ref[block, 0] = key[rows].astype(jnp.bfloat16)
        kv_ref[block, 1] = value[rows].T.astype(jnp.bfloat16)


def first_body(state_ref, gain_ref, wk_ref, wv_ref, normed_ref, kv_ref, w_scr):
    @pl.when(pl.program_id(0) == 0)
    def _():
        w_scr[:, :HD] = wk_ref[...]
        w_scr[:, HD:] = wv_ref[...]

    normed = normalize(state_ref[...].astype(jnp.float32), gain_ref[...])
    normed_ref[...] = normed
    both = dot(normed, w_scr[...])
    store_blocks(kv_ref, both[:, :HD], both[:, HD:])


def first_projection(state, gain, w_key, w_value):
    rows, width = state.shape
    per_tile = TILE // BLK
    return call(
        first_body,
        (rows // TILE,),
        [
            pl.BlockSpec((TILE, width), lambda i: (i, 0)),
            pl.BlockSpec((1, width), lambda i: (0, 0)),
            pl.BlockSpec((width, HD), lambda i: (0, 0)),
            pl.BlockSpec((width, HD), lambda i: (0, 0)),
        ],
        [
            pl.BlockSpec((TILE, width), lambda i: (i, 0)),
            pl.BlockSpec((per_tile, 2, BLK, HD), lambda i: (i, 0, 0, 0)),
        ],
        [
            jax.ShapeDtypeStruct((rows, width), jnp.bfloat16),
            jax.ShapeDtypeStruct((rows // BLK, 2, BLK, HD), jnp.bfloat16),
        ],
        scratch=[pltpu.VMEM((width, 2 * HD), jnp.bfloat16)],
        flops=2 * rows * width * 2 * HD,
        moved=4 * rows * width,
    )(state, gain, w_key, w_value)


def rest_body(heads, normed_ref, wq_ref, wk_ref, wv_ref, *outs):
    normed = normed_ref[...]
    key = dot(normed, wk_ref[:, HD:])
    value = dot(normed, wv_ref[:, HD:])
    for head in range(1, heads):
        cols = slice((head - 1) * HD, head * HD)
        store_blocks(outs[head - 1], key[:, cols], value[:, cols])
    outs[heads - 1][...] = dot(normed, wq_ref[...]).astype(jnp.bfloat16)


def rest_projection(normed, w_query, w_key, w_value):
    rows, width = normed.shape
    local = w_query.shape[1]
    heads = local // HD
    per_tile = TILE // BLK
    full = pl.BlockSpec((width, local), lambda i: (0, 0))
    blocks = pl.BlockSpec((per_tile, 2, BLK, HD), lambda i: (i, 0, 0, 0))
    return call(
        functools.partial(rest_body, heads),
        (rows // TILE,),
        [pl.BlockSpec((TILE, width), lambda i: (i, 0)), full, full, full],
        [blocks] * (heads - 1) + [pl.BlockSpec((TILE, local), lambda i: (i, 0))],
        [jax.ShapeDtypeStruct((rows // BLK, 2, BLK, HD), jnp.bfloat16)] * (heads - 1)
        + [jax.ShapeDtypeStruct((rows, local), jnp.bfloat16)],
        flops=2 * rows * width * (3 * local - 2 * HD),
        moved=2 * rows * width + 6 * width * local,
    )(normed, w_query, w_key, w_value)


def attend_body(blocks, slots, frames, newer, where_ref, counts_ref, q_ref, ck_ref, cv_ref, *rest):
    rest = list(rest)
    last_ref = rest.pop(0) if newer else None
    own, left, right, far_left, far_right, out_ref, window, sem = rest
    index = pl.program_id(0)
    half = blocks // 2

    @pl.when(index == 0)
    def _():
        place = 0
        copies = []
        for piece, length in ((far_left, half), (left, blocks), (own, blocks), (right, blocks), (far_right, half)):
            copies.append(pltpu.make_async_copy(piece, window.at[pl.ds(place, length)], sem.at[len(copies)]))
            place += length
        for copy in copies:
            copy.start()
        for copy in copies:
            copy.wait()

    scale = math.log2(math.e) / math.sqrt(HD)
    live = counts_ref[index]
    query = q_ref[...]
    eye = lax.broadcasted_iota(jnp.int32, (BLK, BLK), 0) == lax.broadcasted_iota(jnp.int32, (BLK, BLK), 1)
    places = [where_ref[index * slots + slot] for slot in range(slots)]
    scores = []
    for slot in range(slots):
        score = lax.dot_general(window[places[slot], 0], query, NT, preferred_element_type=jnp.float32)
        scores.append(jnp.where(slot < live, score, jnp.float32(-1e30)))
    temporal = []
    for frame in range(frames):
        key = last_ref[0, 0] if newer and frame == 0 else ck_ref[frame]
        pairs = lax.dot_general(key, query, NT, preferred_element_type=jnp.float32)
        temporal.append(jnp.sum(jnp.where(eye, pairs, 0.0), axis=0, keepdims=True))
    top = functools.reduce(jnp.maximum, scores).max(axis=0, keepdims=True)
    top = functools.reduce(jnp.maximum, temporal, top)
    weights = [jnp.exp2((score - top) * scale) for score in scores]
    temporal = [jnp.exp2((score - top) * scale) for score in temporal]
    total = functools.reduce(jnp.add, weights).sum(axis=0, keepdims=True)
    total = functools.reduce(jnp.add, temporal, total)
    share = 1.0 / total
    values = jnp.concatenate([window[place, 1] for place in places], axis=1)
    mixed = dot(values, jnp.concatenate([weight.astype(jnp.bfloat16) for weight in weights], axis=0)) * share
    if newer:
        mixed = mixed + last_ref[0, 1].astype(jnp.float32) * (temporal[0] * share)
    skip = 1 if newer else 0
    spread = jnp.concatenate(
        [jnp.where(eye, weight * share, 0.0).astype(jnp.bfloat16) for weight in temporal[skip:]], axis=1
    )
    past = dot(spread, cv_ref[skip:].reshape((frames - skip) * BLK, HD))
    out_ref[...] = (mixed.T + past).astype(jnp.bfloat16)


def attend(head, where_block, counts, queries, cache_key, cache_value, last, pieces):
    rows = queries.shape[0]
    blocks = rows // BLK
    slots = where_block.shape[0] // blocks
    frames = cache_key.shape[0]
    newer = last is not None
    cached = pl.BlockSpec((frames, BLK, HD), lambda i, *_: (0, i, head))
    anywhere = pl.BlockSpec(memory_space=pl.ANY)
    total_blocks = sum(piece.shape[0] for piece in pieces)
    return call(
        functools.partial(attend_body, blocks, slots, frames, newer),
        (blocks,),
        [pl.BlockSpec((BLK, HD), lambda i, *_: (i, head)), cached, cached]
        + ([pl.BlockSpec((1, 2, BLK, HD), lambda i, *_: (i, 0, 0, 0))] if newer else [])
        + [anywhere] * len(pieces),
        pl.BlockSpec((BLK, HD), lambda i, *_: (i, 0)),
        jax.ShapeDtypeStruct((rows, HD), jnp.bfloat16),
        scratch=[
            pltpu.VMEM((total_blocks, 2, BLK, HD), jnp.bfloat16),
            pltpu.SemaphoreType.DMA((len(pieces),)),
        ],
        prefetch=2,
        flops=4 * rows * (slots + frames) * BLK * HD,
        moved=4 * frames * rows * HD + total_blocks * 4 * BLK * HD,
        exps=rows * slots * BLK,
    )(where_block, counts, queries, cache_key, cache_value, *([last] if newer else []), *pieces)


def gather_rows(w_scr, own_ref, others_ref, heads):
    groups = others_ref.shape[1] + 1
    for group in range(groups):
        for at, head in enumerate(heads):
            start = (group * len(heads) + at) * HD
            if group == 0:
                w_scr[start : start + HD] = own_ref[head * HD : (head + 1) * HD]
            else:
                w_scr[start : start + HD] = others_ref[:, group - 1, head].reshape(HD, w_scr.shape[1])


def part_body(heads, count, state_ref, own_ref, others_ref, *rest):
    pieces, (out_ref, w_scr) = rest[:count], rest[count:]

    @pl.when(pl.program_id(0) == 0)
    def _():
        gather_rows(w_scr, own_ref, others_ref, heads)

    attended = jnp.concatenate([piece[...] for piece in pieces], axis=1)
    out_ref[...] = (state_ref[...].astype(jnp.float32) + dot(attended, w_scr[...])).astype(out_ref.dtype)


def add_heads(heads, state, w_own, w_others, pieces, out_dtype):
    rows, width = state.shape
    depth = len(pieces) * HD
    return call(
        functools.partial(part_body, heads, len(pieces)),
        (rows // TILE,),
        [
            pl.BlockSpec((TILE, width), lambda i: (i, 0)),
            pl.BlockSpec(w_own.shape, lambda i: (0, 0)),
            pl.BlockSpec(w_others.shape, lambda i: (0, 0, 0, 0, 0)),
        ]
        + [pl.BlockSpec((TILE, HD), lambda i: (i, 0))] * len(pieces),
        pl.BlockSpec((TILE, width), lambda i: (i, 0)),
        jax.ShapeDtypeStruct((rows, width), out_dtype),
        scratch=[pltpu.VMEM((depth, width), jnp.bfloat16)],
        flops=2 * rows * width * depth,
        moved=6 * rows * width + 2 * depth * width,
    )(state, w_own, w_others, *pieces)


def turn_body(heads, count, part_ref, own_ref, others_ref, gain_ref, wk_ref, wv_ref, *rest):
    pieces, (state_ref, normed_ref, kv_ref, w_scr, kv_scr) = rest[:count], rest[count:]

    @pl.when(pl.program_id(0) == 0)
    def _():
        gather_rows(w_scr, own_ref, others_ref, heads)
        kv_scr[:, :HD] = wk_ref[...]
        kv_scr[:, HD:] = wv_ref[...]

    attended = jnp.concatenate([piece[...] for piece in pieces], axis=1)
    state = (part_ref[...] + dot(attended, w_scr[...])).astype(jnp.bfloat16)
    state_ref[...] = state
    normed = normalize(state.astype(jnp.float32), gain_ref[...])
    normed_ref[...] = normed
    both = dot(normed, kv_scr[...])
    store_blocks(kv_ref, both[:, :HD], both[:, HD:])


def turn(heads, part, w_own, w_others, pieces, gain, w_key, w_value):
    rows, width = part.shape
    depth = len(pieces) * HD
    per_tile = TILE // BLK
    tile = pl.BlockSpec((TILE, width), lambda i: (i, 0))
    return call(
        functools.partial(turn_body, heads, len(pieces)),
        (rows // TILE,),
        [
            tile,
            pl.BlockSpec(w_own.shape, lambda i: (0, 0)),
            pl.BlockSpec(w_others.shape, lambda i: (0, 0, 0, 0, 0)),
            pl.BlockSpec((1, width), lambda i: (0, 0)),
            pl.BlockSpec((width, HD), lambda i: (0, 0)),
            pl.BlockSpec((width, HD), lambda i: (0, 0)),
        ]
        + [pl.BlockSpec((TILE, HD), lambda i: (i, 0))] * len(pieces),
        [tile, tile, pl.BlockSpec((per_tile, 2, BLK, HD), lambda i: (i, 0, 0, 0))],
        [
            jax.ShapeDtypeStruct((rows, width), jnp.bfloat16),
            jax.ShapeDtypeStruct((rows, width), jnp.bfloat16),
            jax.ShapeDtypeStruct((rows // BLK, 2, BLK, HD), jnp.bfloat16),
        ],
        scratch=[pltpu.VMEM((depth, width), jnp.bfloat16), pltpu.VMEM((width, 2 * HD), jnp.bfloat16)],
        flops=2 * rows * width * (depth + 2 * HD),
        moved=8 * rows * width + 2 * depth * width,
    )(part, w_own, w_others, gain, w_key, w_value, *pieces)


def other_groups(w_out):
    count = lax.axis_size("space")
    half = count // 2
    local, width = w_out.shape
    heads = local // HD
    slice_rows = HD // 4
    me = lax.axis_index("space")
    quarter = me % 2 + 2 * (me // half)
    mine = lax.dynamic_index_in_dim(w_out.reshape(heads, 4, slice_rows, width), quarter, 1, keepdims=False)
    fetched = []
    for _ in range(lax.axis_size("head") - 1):
        mine = around(mine, "head")
        fetched.append(mine)
    fours = [[2 * m, 2 * m + 1, half + 2 * m, half + 2 * m + 1] for m in range(half // 2)]
    return lax.all_gather(jnp.stack(fetched), "space", axis_index_groups=fours)


def halo(kv):
    half = kv.shape[0] // 2
    left = shifted(kv, "space", 1)
    right = shifted(kv, "space", -1)
    far_left = shifted(left[half:], "space", 1)
    far_right = shifted(right[:half], "space", -1)
    return kv, left, right, far_left, far_right


def on_device(snapshot, norm_gain, w_query, w_key, w_value, w_out, cache_key, cache_value, pattern, counts):
    tok_rows, width = snapshot.shape
    blocks = tok_rows // BLK
    reach_blocks = blocks + blocks // 2
    block_count_total = blocks * lax.axis_size("space")
    first_block = lax.axis_index("space") * blocks
    heads = w_query.shape[1] // HD
    own_block = jnp.arange(blocks, dtype=jnp.int32)[:, None]
    relative = (pattern - own_block - first_block + block_count_total // 2) % block_count_total
    where_block = (own_block + reach_blocks + relative - block_count_total // 2).reshape(-1)
    gain = norm_gain.reshape(1, width)
    others = other_groups(w_out)
    state = snapshot
    normed, kv_first = first_projection(state, gain, w_key, w_value)
    last_kv = None
    for rollout in range(STEPS):
        kv = [kv_first]
        *kv_rest, queries = rest_projection(normed, w_query, w_key, w_value)
        kv = kv + list(kv_rest)
        came = []
        for head in range(heads):
            pieces = halo(kv[head])
            order = (pieces[0], pieces[1], pieces[2], pieces[3], pieces[4])
            attended = attend(
                head, where_block, counts, queries, cache_key, cache_value, last_kv[head] if last_kv else None, order
            )
            rounds = [attended]
            for _ in range(lax.axis_size("head") - 1):
                rounds.append(around(rounds[-1], "head"))
            came.append(rounds)
        early = list(range(heads - 1))
        groups = lax.axis_size("head")
        part = add_heads(
            early, state, w_out, others, [came[head][group] for group in range(groups) for head in early], jnp.float32
        )
        if rollout + 1 < STEPS:
            state, normed, kv_first = turn([heads - 1], part, w_out, others, came[-1], gain, w_key, w_value)
            last_kv = kv
        else:
            state = add_heads([heads - 1], part, w_out, others, came[-1], jnp.bfloat16)
    return state


def solution(mesh):
    placed = (
        P("space", None),
        P(),
        P(None, "head"),
        P(None, "head"),
        P(None, "head"),
        P("head", None),
        P(None, "space", "head"),
        P(None, "space", "head"),
        P("space", None),
        P("space"),
    )
    return jax.shard_map(
        on_device, mesh=mesh, in_specs=placed, out_specs=P("space", None), check_vma=False
    )
```

```python
import functools
import math

import jax
import jax.numpy as jnp
from jax import lax
from jax.experimental import pallas as pl
from jax.experimental.pallas import tpu as pltpu
from jax.sharding import PartitionSpec as P

HD = 128
BLK = 128
STEPS = 2
TILE = 256
MIB = 1024 * 1024
SCALE = math.log2(math.e) / math.sqrt(HD)


def shifted(value, axis, steps):
    count = lax.axis_size(axis)
    pairs = [(source, (source + steps) % count) for source in range(count)]
    return lax.ppermute(value, axis, pairs)


def around(value, axis):
    count = lax.axis_size(axis)
    order = list(range(0, count, 2)) + list(range(1, count, 2))[::-1]
    onward = [(order[i], order[(i + 1) % count]) for i in range(count)]
    back = [(target, source) for source, target in onward]
    came, ahead, behind = [value], value, value
    for hop in range(count - 1):
        if hop % 2 == 0:
            ahead = lax.ppermute(ahead, axis, onward)
            came.append(ahead)
        else:
            behind = lax.ppermute(behind, axis, back)
            came.append(behind)
    return came


def after(value, *others):
    return lax.optimization_barrier((value,) + others)[0]


def call(body, grid, in_specs, out_specs, out_shape, vmem, scratch=(), prefetch=0, flops=0, moved=0, exps=0):
    return pl.pallas_call(
        body,
        grid_spec=pltpu.PrefetchScalarGridSpec(
            num_scalar_prefetch=prefetch,
            grid=grid,
            in_specs=in_specs,
            out_specs=out_specs,
            scratch_shapes=list(scratch),
        ),
        out_shape=out_shape,
        compiler_params=pltpu.CompilerParams(
            dimension_semantics=("arbitrary",) * len(grid), vmem_limit_bytes=vmem * MIB
        ),
        cost_estimate=pl.CostEstimate(flops=flops, bytes_accessed=moved, transcendentals=exps),
    )


def dot(a, b):
    return jnp.dot(a, b, preferred_element_type=jnp.float32)


def normalize(state, gain):
    meansq = jnp.mean(state * state, axis=-1, keepdims=True)
    return (state * lax.rsqrt(meansq + 1e-05) * gain).astype(jnp.bfloat16)


def store_blocks(kv_ref, key, value):
    for block in range(key.shape[0] // BLK):
        rows = slice(block * BLK, (block + 1) * BLK)
        kv_ref[block, 0] = key[rows].astype(jnp.bfloat16)
        kv_ref[block, 1] = value[rows].T.astype(jnp.bfloat16)


def first_body(state_ref, gain_ref, wk_ref, wv_ref, kv_ref, w_scr):
    @pl.when(pl.program_id(0) == 0)
    def _():
        w_scr[:, :HD] = wk_ref[...]
        w_scr[:, HD:] = wv_ref[...]

    both = dot(normalize(state_ref[...].astype(jnp.float32), gain_ref[...]), w_scr[...])
    store_blocks(kv_ref, both[:, :HD], both[:, HD:])


def first_projection(state, gain, w_key, w_value):
    rows, width = state.shape
    per_tile = TILE // BLK
    return call(
        first_body,
        (rows // TILE,),
        [
            pl.BlockSpec((TILE, width), lambda i: (i, 0)),
            pl.BlockSpec((1, width), lambda i: (0, 0)),
            pl.BlockSpec((width, HD), lambda i: (0, 0)),
            pl.BlockSpec((width, HD), lambda i: (0, 0)),
        ],
        pl.BlockSpec((per_tile, 2, BLK, HD), lambda i: (i, 0, 0, 0)),
        jax.ShapeDtypeStruct((rows // BLK, 2, BLK, HD), jnp.bfloat16),
        12,
        scratch=[pltpu.VMEM((width, 2 * HD), jnp.bfloat16)],
        flops=2 * rows * width * 2 * HD,
        moved=2 * rows * width,
    )(state, gain, w_key, w_value)


def rest_body(heads, state_ref, gain_ref, wq_ref, wk_ref, wv_ref, *outs):
    normed = normalize(state_ref[...].astype(jnp.float32), gain_ref[...])
    key = dot(normed, wk_ref[:, HD:])
    value = dot(normed, wv_ref[:, HD:])
    for head in range(1, heads):
        cols = slice((head - 1) * HD, head * HD)
        store_blocks(outs[head - 1], key[:, cols], value[:, cols])
    query = dot(normed, wq_ref[...])
    for block in range(TILE // BLK):
        for head in range(heads):
            part = query[block * BLK : (block + 1) * BLK, head * HD : (head + 1) * HD]
            outs[heads - 1][block, head] = part.T.astype(jnp.bfloat16)


def rest_projection(state, gain, w_query, w_key, w_value):
    rows, width = state.shape
    local = w_query.shape[1]
    heads = local // HD
    per_tile = TILE // BLK
    full = pl.BlockSpec((width, local), lambda i: (0, 0))
    blocks = pl.BlockSpec((per_tile, 2, BLK, HD), lambda i: (i, 0, 0, 0))
    return call(
        functools.partial(rest_body, heads),
        (rows // TILE,),
        [
            pl.BlockSpec((TILE, width), lambda i: (i, 0)),
            pl.BlockSpec((1, width), lambda i: (0, 0)),
            full,
            full,
            full,
        ],
        [blocks] * (heads - 1) + [pl.BlockSpec((per_tile, heads, HD, BLK), lambda i: (i, 0, 0, 0))],
        [jax.ShapeDtypeStruct((rows // BLK, 2, BLK, HD), jnp.bfloat16)] * (heads - 1)
        + [jax.ShapeDtypeStruct((rows // BLK, heads, HD, BLK), jnp.bfloat16)],
        16,
        flops=2 * rows * width * (3 * local - 2 * HD),
        moved=2 * rows * width + 6 * width * local,
    )(state, gain, w_query, w_key, w_value)


def same_token():
    return lax.broadcasted_iota(jnp.int32, (BLK, BLK), 0) == lax.broadcasted_iota(jnp.int32, (BLK, BLK), 1)


def past_body(frames, heads, newer, qt_ref, ck_ref, cv_ref, *rest):
    last, (acc_ref, stat_ref) = rest[:-2], rest[-2:]
    eye = same_token()
    skip = 1 if newer else 0
    for head in range(heads):
        cols = slice(head * HD, (head + 1) * HD)
        keys = [ck_ref[frame, :, cols] for frame in range(skip, frames)]
        if newer:
            keys = [last[head][0, 0]] + keys
        pairs = dot(jnp.concatenate(keys, axis=0), qt_ref[0, head])
        scores = [
            jnp.sum(jnp.where(eye, pairs[frame * BLK : (frame + 1) * BLK], 0.0), axis=0, keepdims=True)
            for frame in range(frames)
        ]
        top = functools.reduce(jnp.maximum, scores)
        weights = [jnp.exp2((score - top) * SCALE) for score in scores]
        stat_ref[0, head, 0:1] = top
        stat_ref[0, head, 1:2] = functools.reduce(jnp.add, weights)
        spread = jnp.concatenate([jnp.where(eye, weight, 0.0).astype(jnp.bfloat16) for weight in weights[skip:]], axis=1)
        mixed = dot(spread, jnp.concatenate([cv_ref[frame, :, cols] for frame in range(skip, frames)], axis=0)).T
        if newer:
            mixed = mixed + last[head][0, 1].astype(jnp.float32) * weights[0]
        acc_ref[0, head] = mixed


def attend_past(queries, cache_key, cache_value, last):
    blocks, heads = queries.shape[:2]
    frames, rows, local = cache_key.shape
    cached = pl.BlockSpec((frames, BLK, local), lambda i: (0, i, 0))
    return call(
        functools.partial(past_body, frames, heads, len(last) > 0),
        (blocks,),
        [pl.BlockSpec((1, heads, HD, BLK), lambda i: (i, 0, 0, 0)), cached, cached]
        + [pl.BlockSpec((1, 2, BLK, HD), lambda i: (i, 0, 0, 0))] * len(last),
        [
            pl.BlockSpec((1, heads, HD, BLK), lambda i: (i, 0, 0, 0)),
            pl.BlockSpec((1, heads, 2, BLK), lambda i: (i, 0, 0, 0)),
        ],
        [
            jax.ShapeDtypeStruct((blocks, heads, HD, BLK), jnp.float32),
            jax.ShapeDtypeStruct((blocks, heads, 2, BLK), jnp.float32),
        ],
        14,
        flops=4 * rows * frames * BLK * local,
        moved=4 * frames * rows * local,
    )(queries, cache_key, cache_value, *last)


def attend_body(blocks, slots, where_ref, counts_ref, qt_ref, acc_ref, stat_ref, *rest):
    own, left, right, far_left, far_right, out_ref, window, sem = rest
    half = blocks // 2
    place = 0
    copies = []
    for piece, length in ((far_left, half), (left, blocks), (own, blocks), (right, blocks), (far_right, half)):
        copies.append(pltpu.make_async_copy(piece, window.at[pl.ds(place, length)], sem.at[len(copies)]))
        place += length
    for copy in copies:
        copy.start()
    for copy in copies:
        copy.wait()
    for block in range(blocks):
        live = counts_ref[block]
        places = [where_ref[block * slots + slot] for slot in range(slots)]
        pairs = dot(jnp.concatenate([window[at, 0] for at in places], axis=0), qt_ref[block, 0])
        scores = [pairs[:BLK]]
        for slot in range(1, slots):
            score = pairs[slot * BLK : (slot + 1) * BLK]
            scores.append(jnp.where(slot < live, score, jnp.float32(-1e30)))
        past_top = stat_ref[block, 0, 0:1]
        top = jnp.maximum(functools.reduce(jnp.maximum, scores).max(axis=0, keepdims=True), past_top)
        weights = [jnp.exp2((score - top) * SCALE) for score in scores]
        fade = jnp.exp2((past_top - top) * SCALE)
        total = functools.reduce(jnp.add, weights).sum(axis=0, keepdims=True) + stat_ref[block, 0, 1:2] * fade
        share = 1.0 / total
        values = jnp.concatenate([window[at, 1] for at in places], axis=1)
        mixed = dot(values, jnp.concatenate([weight.astype(jnp.bfloat16) for weight in weights], axis=0))
        mixed = mixed * share + acc_ref[block, 0] * (fade * share)
        out_ref[block * BLK : (block + 1) * BLK] = mixed.T.astype(jnp.bfloat16)


def attend(head, where_block, counts, queries, past, stats, pieces):
    blocks = queries.shape[0]
    rows = blocks * BLK
    slots = where_block.shape[0] // blocks
    total_blocks = sum(piece.shape[0] for piece in pieces)
    return call(
        functools.partial(attend_body, blocks, slots),
        (1,),
        [
            pl.BlockSpec((blocks, 1, HD, BLK), lambda i, *_: (0, head, 0, 0)),
            pl.BlockSpec((blocks, 1, HD, BLK), lambda i, *_: (0, head, 0, 0)),
            pl.BlockSpec((blocks, 1, 2, BLK), lambda i, *_: (0, head, 0, 0)),
        ]
        + [pl.BlockSpec(memory_space=pl.ANY)] * len(pieces),
        pl.BlockSpec((rows, HD), lambda i, *_: (0, 0)),
        jax.ShapeDtypeStruct((rows, HD), jnp.bfloat16),
        12,
        scratch=[
            pltpu.VMEM((total_blocks, 2, BLK, HD), jnp.bfloat16),
            pltpu.SemaphoreType.DMA((len(pieces),)),
        ],
        prefetch=2,
        flops=4 * rows * slots * BLK * HD,
        moved=total_blocks * 4 * BLK * HD,
        exps=rows * slots * BLK,
    )(where_block, counts, queries, past, stats, *pieces)


def part_body(count, state_ref, w_ref, *rest):
    pieces, out_ref = rest[:count], rest[count]
    attended = jnp.concatenate([piece[...] for piece in pieces], axis=1)
    out_ref[...] = (state_ref[...].astype(jnp.float32) + dot(attended, w_ref[...])).astype(out_ref.dtype)


def add_heads(state, w_rows, pieces, out_dtype):
    rows, width = state.shape
    return call(
        functools.partial(part_body, len(pieces)),
        (rows // TILE,),
        [pl.BlockSpec((TILE, width), lambda i: (i, 0)), pl.BlockSpec(w_rows.shape, lambda i: (0, 0))]
        + [pl.BlockSpec((TILE, HD), lambda i: (i, 0))] * len(pieces),
        pl.BlockSpec((TILE, width), lambda i: (i, 0)),
        jax.ShapeDtypeStruct((rows, width), out_dtype),
        18,
        flops=2 * rows * width * w_rows.shape[0],
        moved=6 * rows * width + 2 * w_rows.size,
    )(state, w_rows, *pieces)


def turn_body(count, part_ref, w_ref, gain_ref, wk_ref, wv_ref, *rest):
    pieces, (state_ref, kv_ref, kv_scr) = rest[:count], rest[count:]

    @pl.when(pl.program_id(0) == 0)
    def _():
        kv_scr[:, :HD] = wk_ref[...]
        kv_scr[:, HD:] = wv_ref[...]

    attended = jnp.concatenate([piece[...] for piece in pieces], axis=1)
    state = (part_ref[...] + dot(attended, w_ref[...])).astype(jnp.bfloat16)
    state_ref[...] = state
    both = dot(normalize(state.astype(jnp.float32), gain_ref[...]), kv_scr[...])
    store_blocks(kv_ref, both[:, :HD], both[:, HD:])


def turn(part, w_rows, pieces, gain, w_key, w_value):
    rows, width = part.shape
    per_tile = TILE // BLK
    tile = pl.BlockSpec((TILE, width), lambda i: (i, 0))
    return call(
        functools.partial(turn_body, len(pieces)),
        (rows // TILE,),
        [
            tile,
            pl.BlockSpec(w_rows.shape, lambda i: (0, 0)),
            pl.BlockSpec((1, width), lambda i: (0, 0)),
            pl.BlockSpec((width, HD), lambda i: (0, 0)),
            pl.BlockSpec((width, HD), lambda i: (0, 0)),
        ]
        + [pl.BlockSpec((TILE, HD), lambda i: (i, 0))] * len(pieces),
        [tile, pl.BlockSpec((per_tile, 2, BLK, HD), lambda i: (i, 0, 0, 0))],
        [
            jax.ShapeDtypeStruct((rows, width), jnp.bfloat16),
            jax.ShapeDtypeStruct((rows // BLK, 2, BLK, HD), jnp.bfloat16),
        ],
        18,
        scratch=[pltpu.VMEM((width, 2 * HD), jnp.bfloat16)],
        flops=2 * rows * width * (w_rows.shape[0] + 2 * HD),
        moved=6 * rows * width + 2 * w_rows.size,
    )(part, w_rows, gain, w_key, w_value, *pieces)


def all_rows(w_out, start):
    count = lax.axis_size("space")
    half = count // 2
    local, width = w_out.shape
    heads = local // HD
    me = lax.axis_index("space")
    quarter = me % 2 + 2 * (me // half)
    own = w_out.reshape(heads, 4, HD // 4, width)
    mine = lax.dynamic_index_in_dim(own, quarter, 1, keepdims=False)
    fetched = jnp.stack(around(after(mine, start), "head")[1:])
    fours = [[2 * m, 2 * m + 1, half + 2 * m, half + 2 * m + 1] for m in range(half // 2)]
    others = lax.all_gather(fetched, "space", axis_index_groups=fours)
    others = others.transpose(1, 2, 0, 3, 4).reshape(-1, heads, HD, width)
    return jnp.concatenate([w_out.reshape(1, heads, HD, width), others])


def on_device(snapshot, norm_gain, w_query, w_key, w_value, w_out, cache_key, cache_value, pattern, counts):
    tok_rows, width = snapshot.shape
    blocks = tok_rows // BLK
    half = blocks // 2
    reach_blocks = blocks + half
    block_count_total = blocks * lax.axis_size("space")
    first_block = lax.axis_index("space") * blocks
    heads = w_query.shape[1] // HD
    own_block = jnp.arange(blocks, dtype=jnp.int32)[:, None]
    relative = (pattern - own_block - first_block + block_count_total // 2) % block_count_total
    where_block = (own_block + reach_blocks + relative - block_count_total // 2).reshape(-1)
    gain = norm_gain.reshape(1, width)
    state = snapshot
    kv_first = first_projection(state, gain, w_key, w_value)
    rows_of = all_rows(w_out, kv_first)
    w_early = rows_of[:, : heads - 1].reshape(-1, width)
    w_last = rows_of[:, heads - 1].reshape(-1, width)
    last = []
    for rollout in range(STEPS):
        *kv_rest, queries = rest_projection(state, gain, w_query, w_key, w_value)
        kv = [kv_first] + list(kv_rest)
        past, stats = attend_past(queries, cache_key, cache_value, last)
        near = []
        for head in range(heads):
            sent = kv[head] if head < 2 else after(kv[head], *near[head - 2])
            near.append((shifted(sent, "space", 1), shifted(sent, "space", -1)))
        came = []
        for head in range(heads):
            left, right = near[head]
            pieces = (kv[head], left, right, shifted(left[half:], "space", 1), shifted(right[:half], "space", -1))
            came.append(around(attend(head, where_block, counts, queries, past, stats, pieces), "head"))
        early = [piece for group in zip(*came[:-1], strict=True) for piece in group]
        part = add_heads(state, w_early, early, jnp.float32)
        if rollout + 1 < STEPS:
            state, kv_first = turn(part, w_last, came[-1], gain, w_key, w_value)
            last = kv
        else:
            state = add_heads(part, w_last, came[-1], jnp.bfloat16)
    return state


def solution(mesh):
    placed = (
        P("space", None),
        P(),
        P(None, "head"),
        P(None, "head"),
        P(None, "head"),
        P("head", None),
        P(None, "space", "head"),
        P(None, "space", "head"),
        P("space", None),
        P("space"),
    )
    return jax.shard_map(
        on_device, mesh=mesh, in_specs=placed, out_specs=P("space", None), check_vma=False
    )
```

```python
import functools
import math

import jax
import jax.numpy as jnp
from jax import lax
from jax.experimental import pallas as pl
from jax.experimental.pallas import tpu as pltpu
from jax.sharding import PartitionSpec as P

HD = 128
BLK = 128
STEPS = 2
TILE = 256
MIB = 1024 * 1024
SCALE = math.log2(math.e) / math.sqrt(HD)


def shifted(value, axis, steps):
    count = lax.axis_size(axis)
    pairs = [(source, (source + steps) % count) for source in range(count)]
    return lax.ppermute(value, axis, pairs)


def around(value, axis, then=()):
    count = lax.axis_size(axis)
    order = list(range(0, count, 2)) + list(range(1, count, 2))[::-1]
    onward = [(order[i], order[(i + 1) % count]) for i in range(count)]
    back = [(target, source) for source, target in onward]
    came, ahead, behind = [value], value, value
    for hop in range(count - 1):
        if hop == 2 and then:
            ahead = after(ahead, *then)
        if hop % 2 == 0:
            ahead = lax.ppermute(ahead, axis, onward)
            came.append(ahead)
        else:
            behind = lax.ppermute(behind, axis, back)
            came.append(behind)
    return came


def after(value, *others):
    return lax.optimization_barrier((value,) + others)[0]


def call(body, grid, in_specs, out_specs, out_shape, vmem, scratch=(), prefetch=0, flops=0, moved=0, exps=0):
    return pl.pallas_call(
        body,
        grid_spec=pltpu.PrefetchScalarGridSpec(
            num_scalar_prefetch=prefetch,
            grid=grid,
            in_specs=in_specs,
            out_specs=out_specs,
            scratch_shapes=list(scratch),
        ),
        out_shape=out_shape,
        compiler_params=pltpu.CompilerParams(
            dimension_semantics=("arbitrary",) * len(grid), vmem_limit_bytes=vmem * MIB
        ),
        cost_estimate=pl.CostEstimate(flops=flops, bytes_accessed=moved, transcendentals=exps),
    )


def dot(a, b):
    return jnp.dot(a, b, preferred_element_type=jnp.float32)


def normalize(state, gain):
    meansq = jnp.mean(state * state, axis=-1, keepdims=True)
    return (state * lax.rsqrt(meansq + 1e-05) * gain).astype(jnp.bfloat16)


def store_blocks(kv_ref, key, value):
    for block in range(key.shape[0] // BLK):
        rows = slice(block * BLK, (block + 1) * BLK)
        kv_ref[block, 0] = key[rows].astype(jnp.bfloat16)
        kv_ref[block, 1] = value[rows].T.astype(jnp.bfloat16)


def first_body(state_ref, gain_ref, wk_ref, wv_ref, kv_ref, w_scr):
    @pl.when(pl.program_id(0) == 0)
    def _():
        w_scr[:, :HD] = wk_ref[...]
        w_scr[:, HD:] = wv_ref[...]

    both = dot(normalize(state_ref[...].astype(jnp.float32), gain_ref[...]), w_scr[...])
    store_blocks(kv_ref, both[:, :HD], both[:, HD:])


def first_projection(state, gain, w_key, w_value):
    rows, width = state.shape
    per_tile = TILE // BLK
    return call(
        first_body,
        (rows // TILE,),
        [
            pl.BlockSpec((TILE, width), lambda i: (i, 0)),
            pl.BlockSpec((1, width), lambda i: (0, 0)),
            pl.BlockSpec((width, HD), lambda i: (0, 0)),
            pl.BlockSpec((width, HD), lambda i: (0, 0)),
        ],
        pl.BlockSpec((per_tile, 2, BLK, HD), lambda i: (i, 0, 0, 0)),
        jax.ShapeDtypeStruct((rows // BLK, 2, BLK, HD), jnp.bfloat16),
        60,
        scratch=[pltpu.VMEM((width, 2 * HD), jnp.bfloat16)],
        flops=2 * rows * width * 2 * HD,
        moved=2 * rows * width,
    )(state, gain, w_key, w_value)


def rest_body(heads, state_ref, gain_ref, wq_ref, wk_ref, wv_ref, *outs):
    normed = normalize(state_ref[...].astype(jnp.float32), gain_ref[...])
    key = dot(normed, wk_ref[:, HD:])
    value = dot(normed, wv_ref[:, HD:])
    for head in range(1, heads):
        cols = slice((head - 1) * HD, head * HD)
        store_blocks(outs[head - 1], key[:, cols], value[:, cols])
    query = dot(normed, wq_ref[...])
    for block in range(TILE // BLK):
        for head in range(heads):
            part = query[block * BLK : (block + 1) * BLK, head * HD : (head + 1) * HD]
            outs[heads - 1][block, head] = part.T.astype(jnp.bfloat16)


def rest_projection(state, gain, w_query, w_key, w_value):
    rows, width = state.shape
    local = w_query.shape[1]
    heads = local // HD
    per_tile = TILE // BLK
    full = pl.BlockSpec((width, local), lambda i: (0, 0))
    blocks = pl.BlockSpec((per_tile, 2, BLK, HD), lambda i: (i, 0, 0, 0))
    return call(
        functools.partial(rest_body, heads),
        (rows // TILE,),
        [
            pl.BlockSpec((TILE, width), lambda i: (i, 0)),
            pl.BlockSpec((1, width), lambda i: (0, 0)),
            full,
            full,
            full,
        ],
        [blocks] * (heads - 1) + [pl.BlockSpec((per_tile, heads, HD, BLK), lambda i: (i, 0, 0, 0))],
        [jax.ShapeDtypeStruct((rows // BLK, 2, BLK, HD), jnp.bfloat16)] * (heads - 1)
        + [jax.ShapeDtypeStruct((rows // BLK, heads, HD, BLK), jnp.bfloat16)],
        16,
        flops=2 * rows * width * (3 * local - 2 * HD),
        moved=2 * rows * width + 6 * width * local,
    )(state, gain, w_query, w_key, w_value)


def same_token():
    return lax.broadcasted_iota(jnp.int32, (BLK, BLK), 0) == lax.broadcasted_iota(jnp.int32, (BLK, BLK), 1)


def past_body(frames, heads, newer, qt_ref, ck_ref, cv_ref, *rest):
    last, (acc_ref, stat_ref) = rest[:-2], rest[-2:]
    eye = same_token()
    none = jnp.zeros((BLK, BLK), jnp.bfloat16)
    for block in range(qt_ref.shape[0]):
        rows = slice(block * BLK, (block + 1) * BLK)
        for head in range(heads):
            cols = slice(head * HD, (head + 1) * HD)
            keys = [ck_ref[frame, rows, cols] for frame in range(frames)]
            if newer:
                keys[0] = last[head][block, 0]
            pairs = dot(jnp.concatenate(keys, axis=0), qt_ref[block, head])
            scores = [
                jnp.sum(jnp.where(eye, pairs[frame * BLK : (frame + 1) * BLK], 0.0), axis=0, keepdims=True)
                for frame in range(frames)
            ]
            top = functools.reduce(jnp.maximum, scores)
            weights = [jnp.exp2((score - top) * SCALE) for score in scores]
            stat_ref[block, head, 0:1] = top
            stat_ref[block, head, 1:2] = functools.reduce(jnp.add, weights)
            spread = [jnp.where(eye, weight, 0.0).astype(jnp.bfloat16) for weight in weights]
            if newer:
                spread[0] = none
            values = jnp.concatenate([cv_ref[frame, rows, cols] for frame in range(frames)], axis=0)
            mixed = dot(jnp.concatenate(spread, axis=1), values).T
            if newer:
                mixed = mixed + last[head][block, 1].astype(jnp.float32) * weights[0]
            acc_ref[block, head] = mixed


def attend_past(queries, cache_key, cache_value, last):
    blocks, heads = queries.shape[:2]
    frames, rows, local = cache_key.shape
    per_tile = TILE // BLK
    cached = pl.BlockSpec((frames, TILE, local), lambda i: (0, i, 0))
    return call(
        functools.partial(past_body, frames, heads, len(last) > 0),
        (blocks // per_tile,),
        [pl.BlockSpec((per_tile, heads, HD, BLK), lambda i: (i, 0, 0, 0)), cached, cached]
        + [pl.BlockSpec((per_tile, 2, BLK, HD), lambda i: (i, 0, 0, 0))] * len(last),
        [
            pl.BlockSpec((per_tile, heads, HD, BLK), lambda i: (i, 0, 0, 0)),
            pl.BlockSpec((per_tile, heads, 2, BLK), lambda i: (i, 0, 0, 0)),
        ],
        [
            jax.ShapeDtypeStruct((blocks, heads, HD, BLK), jnp.float32),
            jax.ShapeDtypeStruct((blocks, heads, 2, BLK), jnp.float32),
        ],
        20,
        flops=4 * rows * frames * BLK * local,
        moved=4 * frames * rows * local,
    )(queries, cache_key, cache_value, *last)


def attend_body(blocks, slots, where_ref, counts_ref, qt_ref, acc_ref, stat_ref, *rest):
    own, left, right, far_left, far_right, out_ref, window, sem = rest
    half = blocks // 2
    place = 0
    copies = []
    for piece, length in ((far_left, half), (left, blocks), (own, blocks), (right, blocks), (far_right, half)):
        copies.append(pltpu.make_async_copy(piece, window.at[pl.ds(place, length)], sem.at[len(copies)]))
        place += length
    for copy in copies:
        copy.start()
    for copy in copies:
        copy.wait()
    for block in range(blocks):
        live = counts_ref[block]
        places = [where_ref[block * slots + slot] for slot in range(slots)]
        pairs = dot(jnp.concatenate([window[at, 0] for at in places], axis=0), qt_ref[block, 0])
        scores = [pairs[:BLK]]
        for slot in range(1, slots):
            score = pairs[slot * BLK : (slot + 1) * BLK]
            scores.append(jnp.where(slot < live, score, jnp.float32(-1e30)))
        past_top = stat_ref[block, 0, 0:1]
        top = jnp.maximum(functools.reduce(jnp.maximum, scores).max(axis=0, keepdims=True), past_top)
        weights = [jnp.exp2((score - top) * SCALE) for score in scores]
        fade = jnp.exp2((past_top - top) * SCALE)
        total = functools.reduce(jnp.add, weights).sum(axis=0, keepdims=True) + stat_ref[block, 0, 1:2] * fade
        share = 1.0 / total
        values = jnp.concatenate([window[at, 1] for at in places], axis=1)
        mixed = dot(values, jnp.concatenate([weight.astype(jnp.bfloat16) for weight in weights], axis=0))
        mixed = mixed * share + acc_ref[block, 0] * (fade * share)
        out_ref[block * BLK : (block + 1) * BLK] = mixed.T.astype(jnp.bfloat16)


def attend(head, where_block, counts, queries, past, stats, pieces):
    blocks = queries.shape[0]
    rows = blocks * BLK
    slots = where_block.shape[0] // blocks
    total_blocks = sum(piece.shape[0] for piece in pieces)
    return call(
        functools.partial(attend_body, blocks, slots),
        (1,),
        [
            pl.BlockSpec((blocks, 1, HD, BLK), lambda i, *_: (0, head, 0, 0)),
            pl.BlockSpec((blocks, 1, HD, BLK), lambda i, *_: (0, head, 0, 0)),
            pl.BlockSpec((blocks, 1, 2, BLK), lambda i, *_: (0, head, 0, 0)),
        ]
        + [pl.BlockSpec(memory_space=pl.ANY)] * len(pieces),
        pl.BlockSpec((rows, HD), lambda i, *_: (0, 0)),
        jax.ShapeDtypeStruct((rows, HD), jnp.bfloat16),
        12,
        scratch=[
            pltpu.VMEM((total_blocks, 2, BLK, HD), jnp.bfloat16),
            pltpu.SemaphoreType.DMA((len(pieces),)),
        ],
        prefetch=2,
        flops=4 * rows * slots * BLK * HD,
        moved=total_blocks * 4 * BLK * HD,
        exps=rows * slots * BLK,
    )(where_block, counts, queries, past, stats, *pieces)


def part_body(count, state_ref, w_ref, *rest):
    pieces, out_ref = rest[:count], rest[count]
    attended = jnp.concatenate([piece[...] for piece in pieces], axis=1)
    out_ref[...] = (state_ref[...].astype(jnp.float32) + dot(attended, w_ref[...])).astype(out_ref.dtype)


def add_heads(state, w_rows, pieces, out_dtype):
    rows, width = state.shape
    return call(
        functools.partial(part_body, len(pieces)),
        (rows // TILE,),
        [pl.BlockSpec((TILE, width), lambda i: (i, 0)), pl.BlockSpec(w_rows.shape, lambda i: (0, 0))]
        + [pl.BlockSpec((TILE, HD), lambda i: (i, 0))] * len(pieces),
        pl.BlockSpec((TILE, width), lambda i: (i, 0)),
        jax.ShapeDtypeStruct((rows, width), out_dtype),
        18,
        flops=2 * rows * width * w_rows.shape[0],
        moved=6 * rows * width + 2 * w_rows.size,
    )(state, w_rows, *pieces)


def turn_body(count, part_ref, w_ref, gain_ref, wk_ref, wv_ref, *rest):
    pieces, (state_ref, kv_ref, kv_scr) = rest[:count], rest[count:]

    @pl.when(pl.program_id(0) == 0)
    def _():
        kv_scr[:, :HD] = wk_ref[...]
        kv_scr[:, HD:] = wv_ref[...]

    attended = jnp.concatenate([piece[...] for piece in pieces], axis=1)
    state = (part_ref[...] + dot(attended, w_ref[...])).astype(jnp.bfloat16)
    state_ref[...] = state
    both = dot(normalize(state.astype(jnp.float32), gain_ref[...]), kv_scr[...])
    store_blocks(kv_ref, both[:, :HD], both[:, HD:])


def turn(part, w_rows, pieces, gain, w_key, w_value):
    rows, width = part.shape
    per_tile = TILE // BLK
    tile = pl.BlockSpec((TILE, width), lambda i: (i, 0))
    return call(
        functools.partial(turn_body, len(pieces)),
        (rows // TILE,),
        [
            tile,
            pl.BlockSpec(w_rows.shape, lambda i: (0, 0)),
            pl.BlockSpec((1, width), lambda i: (0, 0)),
            pl.BlockSpec((width, HD), lambda i: (0, 0)),
            pl.BlockSpec((width, HD), lambda i: (0, 0)),
        ]
        + [pl.BlockSpec((TILE, HD), lambda i: (i, 0))] * len(pieces),
        [tile, pl.BlockSpec((per_tile, 2, BLK, HD), lambda i: (i, 0, 0, 0))],
        [
            jax.ShapeDtypeStruct((rows, width), jnp.bfloat16),
            jax.ShapeDtypeStruct((rows // BLK, 2, BLK, HD), jnp.bfloat16),
        ],
        18,
        scratch=[pltpu.VMEM((width, 2 * HD), jnp.bfloat16)],
        flops=2 * rows * width * (w_rows.shape[0] + 2 * HD),
        moved=6 * rows * width + 2 * w_rows.size,
    )(part, w_rows, gain, w_key, w_value, *pieces)


def all_rows(w_out, start, then):
    count = lax.axis_size("space")
    half = count // 2
    local, width = w_out.shape
    heads = local // HD
    me = lax.axis_index("space")
    quarter = me % 2 + 2 * (me // half)
    own = w_out.reshape(heads, 4, HD // 4, width)
    mine = lax.dynamic_index_in_dim(own, quarter, 1, keepdims=False)
    fetched = jnp.stack(around(after(mine, start), "head", then)[1:])
    fours = [[2 * m, 2 * m + 1, half + 2 * m, half + 2 * m + 1] for m in range(half // 2)]
    others = lax.all_gather(fetched, "space", axis_index_groups=fours)
    others = others.transpose(1, 2, 0, 3, 4).reshape(-1, heads, HD, width)
    return jnp.concatenate([w_out.reshape(1, heads, HD, width), others])


def on_device(snapshot, norm_gain, w_query, w_key, w_value, w_out, cache_key, cache_value, pattern, counts):
    tok_rows, width = snapshot.shape
    blocks = tok_rows // BLK
    half = blocks // 2
    reach_blocks = blocks + half
    block_count_total = blocks * lax.axis_size("space")
    first_block = lax.axis_index("space") * blocks
    heads = w_query.shape[1] // HD
    own_block = jnp.arange(blocks, dtype=jnp.int32)[:, None]
    relative = (pattern - own_block - first_block + block_count_total // 2) % block_count_total
    where_block = (own_block + reach_blocks + relative - block_count_total // 2).reshape(-1)
    gain = norm_gain.reshape(1, width)
    state = snapshot
    kv_first = first_projection(state, gain, w_key, w_value)
    rows_of = None
    last = []
    for rollout in range(STEPS):
        near = [(shifted(kv_first, "space", 1), shifted(kv_first, "space", -1))]
        *kv_rest, queries = rest_projection(state, gain, w_query, w_key, w_value)
        kv = [kv_first] + list(kv_rest)
        past, stats = attend_past(queries, cache_key, cache_value, last)
        came = []
        for head in range(heads):
            left, right = near[head]
            if head == 0:
                left, right = after(left, past), after(right, past)
            if rows_of is None:
                rows_of = all_rows(w_out, kv_rest[-1], (left, right))
            far = (shifted(left[half:], "space", 1), shifted(right[:half], "space", -1))
            if head + 1 < heads:
                ready = near[0] if head == 0 else (*near[head], *came[head - 1][:1])
                sent = after(kv[head + 1], *ready)
                near.append((shifted(sent, "space", 1), shifted(sent, "space", -1)))
            attended = attend(head, where_block, counts, queries, past, stats, (kv[head], left, right, *far))
            came.append(around(attended, "head"))
        if rollout == 0:
            w_early = rows_of[:, : heads - 1].reshape(-1, width)
            w_last = rows_of[:, heads - 1].reshape(-1, width)
        early = [piece for group in zip(*came[:-1], strict=True) for piece in group]
        part = add_heads(state, w_early, early, jnp.float32)
        if rollout + 1 < STEPS:
            state, kv_first = turn(part, w_last, came[-1], gain, w_key, w_value)
            last = kv
        else:
            state = add_heads(part, w_last, came[-1], jnp.bfloat16)
    return state


def solution(mesh):
    placed = (
        P("space", None),
        P(),
        P(None, "head"),
        P(None, "head"),
        P(None, "head"),
        P("head", None),
        P(None, "space", "head"),
        P(None, "space", "head"),
        P("space", None),
        P("space"),
    )
    return jax.shard_map(
        on_device, mesh=mesh, in_specs=placed, out_specs=P("space", None), check_vma=False
    )
```

```python
import functools
import math

import jax
import jax.numpy as jnp
from jax import lax
from jax.experimental import pallas as pl
from jax.experimental.pallas import tpu as pltpu
from jax.sharding import PartitionSpec as P

HD = 128
BLK = 128
STEPS = 2
TILE = 256
COST = 3.0
R1PIN = 3
ATT_COST = 0.0
PART_COST = 0.0
PAST_VMEM = 52
REST_VMEM = (62, 16)
CHUNKS = ((0,), (1,), (2,))
MIB = 1024 * 1024
SCALE = math.log2(math.e) / math.sqrt(HD)


def sent(value, to):
    count = lax.axis_size("space")
    return lax.ppermute(value, "space", [(i, to(i, count) % count) for i in range(count)])


def across(i, count):
    return i + 1 if i % 2 else i - 1


def beyond(i, count):
    return i - 2 if i % 2 else i + 2


def beside(i, count):
    return i ^ 1


def opposite(i, count):
    return i + count // 2


def turned(value, axis, hops):
    count = lax.axis_size(axis)
    order = list(range(0, count, 2)) + list(range(1, count, 2))[::-1]
    return lax.ppermute(value, axis, [(order[i], order[(i + hops) % count]) for i in range(count)])


def around(value, axis, then=()):
    came = [value]
    for hop in range(1, lax.axis_size(axis)):
        sign = 1 if hop % 2 == 1 else -1
        came.append(turned(came[0] if hop <= 2 else after(came[hop - 2], *then), axis, sign))
    return came


def after(value, *others):
    return lax.optimization_barrier((value,) + others)[0]


def call(body, grid, in_specs, out_specs, out_shape, vmem, scratch=(), prefetch=0, micros=0.0):
    return pl.pallas_call(
        body,
        grid_spec=pltpu.PrefetchScalarGridSpec(
            num_scalar_prefetch=prefetch,
            grid=grid,
            in_specs=in_specs,
            out_specs=out_specs,
            scratch_shapes=list(scratch),
        ),
        out_shape=out_shape,
        compiler_params=pltpu.CompilerParams(
            dimension_semantics=("arbitrary",) * len(grid), vmem_limit_bytes=vmem * MIB
        ),
        cost_estimate=pl.CostEstimate(flops=int(COST * micros * 1.15e9), bytes_accessed=0, transcendentals=0),
    )


def dot(a, b):
    return jnp.dot(a, b, preferred_element_type=jnp.float32)


def normalize(state, gain):
    meansq = jnp.mean(state * state, axis=-1, keepdims=True)
    return (state * lax.rsqrt(meansq + 1e-05) * gain).astype(jnp.bfloat16)


def store_blocks(kv_ref, at, key, value):
    for block in range(key.shape[0] // BLK):
        rows = slice(block * BLK, (block + 1) * BLK)
        kv_ref[block, at, 0] = key[rows].astype(jnp.bfloat16)
        kv_ref[block, at, 1] = value[rows].T.astype(jnp.bfloat16)


def first_body(state_ref, gain_ref, wk_ref, wv_ref, kv_ref, w_scr):
    @pl.when(pl.program_id(0) == 0)
    def _():
        w_scr[:, :HD] = wk_ref[...]
        w_scr[:, HD:] = wv_ref[...]

    both = dot(normalize(state_ref[...].astype(jnp.float32), gain_ref[...]), w_scr[...])
    store_blocks(kv_ref, 0, both[:, :HD], both[:, HD:])


def first_projection(state, gain, w_key, w_value):
    rows, width = state.shape
    per_tile = TILE // BLK
    return call(
        first_body,
        (rows // TILE,),
        [
            pl.BlockSpec((TILE, width), lambda i: (i, 0)),
            pl.BlockSpec((width,), lambda i: (0,)),
            pl.BlockSpec((width, HD), lambda i: (0, 0)),
            pl.BlockSpec((width, HD), lambda i: (0, 0)),
        ],
        pl.BlockSpec((per_tile, 1, 2, BLK, HD), lambda i: (i, 0, 0, 0, 0)),
        jax.ShapeDtypeStruct((rows // BLK, 1, 2, BLK, HD), jnp.bfloat16),
        60,
        scratch=[pltpu.VMEM((width, 2 * HD), jnp.bfloat16)],
        micros=5.0,
    )(state, gain, w_key, w_value)


def rest_body(heads, state_ref, gain_ref, wq_ref, wk_ref, wv_ref, *outs):
    normed = normalize(state_ref[...].astype(jnp.float32), gain_ref[...])
    key = dot(normed, wk_ref[:, HD:])
    value = dot(normed, wv_ref[:, HD:])
    for chunk, kv_ref in zip(CHUNKS[1:], outs, strict=False):
        for at, head in enumerate(chunk):
            cols = slice((head - 1) * HD, head * HD)
            store_blocks(kv_ref, at, key[:, cols], value[:, cols])
    query = dot(normed, wq_ref[...])
    for block in range(TILE // BLK):
        for head in range(heads):
            part = query[block * BLK : (block + 1) * BLK, head * HD : (head + 1) * HD]
            outs[-1][block, head] = part.T.astype(jnp.bfloat16)


def rest_projection(state, gain, w_query, w_key, w_value, vmem):
    rows, width = state.shape
    local = w_query.shape[1]
    heads = local // HD
    per_tile = TILE // BLK
    full = pl.BlockSpec((width, local), lambda i: (0, 0))
    return call(
        functools.partial(rest_body, heads),
        (rows // TILE,),
        [
            pl.BlockSpec((TILE, width), lambda i: (i, 0)),
            pl.BlockSpec((width,), lambda i: (0,)),
            full,
            full,
            full,
        ],
        [pl.BlockSpec((per_tile, len(c), 2, BLK, HD), lambda i: (i, 0, 0, 0, 0)) for c in CHUNKS[1:]]
        + [pl.BlockSpec((per_tile, heads, HD, BLK), lambda i: (i, 0, 0, 0))],
        [jax.ShapeDtypeStruct((rows // BLK, len(c), 2, BLK, HD), jnp.bfloat16) for c in CHUNKS[1:]]
        + [jax.ShapeDtypeStruct((rows // BLK, heads, HD, BLK), jnp.bfloat16)],
        vmem,
        micros=5.0,
    )(state, gain, w_query, w_key, w_value)


def same_token():
    return lax.broadcasted_iota(jnp.int32, (BLK, BLK), 0) == lax.broadcasted_iota(jnp.int32, (BLK, BLK), 1)


def past_body(frames, heads, newer, qt_ref, ck_hbm, cv_hbm, *rest):
    last, (acc_ref, stat_ref, slots, sems) = rest[:-4], rest[-4:]
    place = {head: (c, at) for c, chunk in enumerate(CHUNKS) for at, head in enumerate(chunk)}
    tile = pl.program_id(0)

    def copies(tile):
        rows = pl.ds(pl.multiple_of(tile * TILE, TILE), TILE)
        return [
            pltpu.make_async_copy(cache.at[:, rows], slots.at[tile, which], sems.at[tile, which])
            for which, cache in enumerate((ck_hbm, cv_hbm))
        ]

    @pl.when(tile == 0)
    def _():
        for ahead in range(slots.shape[0]):
            for copy in copies(ahead):
                copy.start()

    for copy in copies(tile):
        copy.wait()
    ck_ref, cv_ref = (slots.at[tile, which] for which in range(2))
    eye = same_token()
    none = jnp.zeros((BLK, BLK), jnp.bfloat16)
    for block in range(qt_ref.shape[0]):
        rows = slice(block * BLK, (block + 1) * BLK)
        for head in range(heads):
            cols = slice(head * HD, (head + 1) * HD)
            keys = [ck_ref[frame, rows, cols] for frame in range(frames)]
            if newer:
                keys[0] = last[place[head][0]][block, place[head][1], 0]
            pairs = dot(jnp.concatenate(keys, axis=0), qt_ref[block, head])
            scores = [
                jnp.sum(jnp.where(eye, pairs[frame * BLK : (frame + 1) * BLK], 0.0), axis=0, keepdims=True)
                for frame in range(frames)
            ]
            top = functools.reduce(jnp.maximum, scores)
            weights = [jnp.exp2((score - top) * SCALE) for score in scores]
            stat_ref[block, head, 0:1] = top
            stat_ref[block, head, 1:2] = functools.reduce(jnp.add, weights)
            spread = [jnp.where(eye, weight, 0.0).astype(jnp.bfloat16) for weight in weights]
            if newer:
                spread[0] = none
            values = jnp.concatenate([cv_ref[frame, rows, cols] for frame in range(frames)], axis=0)
            mixed = dot(jnp.concatenate(spread, axis=1), values).T
            if newer:
                mixed = mixed + last[place[head][0]][block, place[head][1], 1].astype(jnp.float32) * weights[0]
            acc_ref[block, head] = mixed


def attend_past(queries, cache_key, cache_value, last):
    blocks, heads = queries.shape[:2]
    frames, rows, local = cache_key.shape
    per_tile = TILE // BLK
    cached = pl.BlockSpec(memory_space=pltpu.HBM)
    return call(
        functools.partial(past_body, frames, heads, len(last) > 0),
        (blocks // per_tile,),
        [pl.BlockSpec((per_tile, heads, HD, BLK), lambda i: (i, 0, 0, 0)), cached, cached]
        + [pl.BlockSpec((per_tile, *piece.shape[1:]), lambda i: (i, 0, 0, 0, 0)) for piece in last],
        [
            pl.BlockSpec((per_tile, heads, HD, BLK), lambda i: (i, 0, 0, 0)),
            pl.BlockSpec((per_tile, heads, 2, BLK), lambda i: (i, 0, 0, 0)),
        ],
        [
            jax.ShapeDtypeStruct((blocks, heads, HD, BLK), jnp.float32),
            jax.ShapeDtypeStruct((blocks, heads, 2, BLK), jnp.float32),
        ],
        PAST_VMEM,
        scratch=[
            pltpu.VMEM((blocks // per_tile, 2, frames, TILE, local), jnp.bfloat16),
            pltpu.SemaphoreType.DMA((blocks // per_tile, 2)),
        ],
        micros=6.0,
    )(queries, cache_key, cache_value, *last)


def attend_body(blocks, slots, inner, where_ref, counts_ref, qt_ref, acc_ref, stat_ref, *rest):
    pieces, (out_ref, window, sem) = rest[:-3], rest[-3:]
    place = 0
    copies = []
    for piece in pieces:
        copies.append(pltpu.make_async_copy(piece, window.at[pl.ds(place, piece.shape[0])], sem.at[len(copies)]))
        place += piece.shape[0]
    for copy in copies:
        copy.start()
    for copy in copies:
        copy.wait()
    for block in range(blocks):
        live = counts_ref[block]
        places = [where_ref[block * slots + slot] for slot in range(slots)]
        for at in range(inner):
            pairs = dot(jnp.concatenate([window[p, at, 0] for p in places], axis=0), qt_ref[block, at])
            scores = [pairs[:BLK]]
            for slot in range(1, slots):
                score = pairs[slot * BLK : (slot + 1) * BLK]
                scores.append(jnp.where(slot < live, score, jnp.float32(-1e30)))
            past_top = stat_ref[block, at, 0:1]
            top = jnp.maximum(functools.reduce(jnp.maximum, scores).max(axis=0, keepdims=True), past_top)
            weights = [jnp.exp2((score - top) * SCALE) for score in scores]
            fade = jnp.exp2((past_top - top) * SCALE)
            total = functools.reduce(jnp.add, weights).sum(axis=0, keepdims=True) + stat_ref[block, at, 1:2] * fade
            share = 1.0 / total
            values = jnp.concatenate([window[p, at, 1] for p in places], axis=1)
            mixed = dot(values, jnp.concatenate([weight.astype(jnp.bfloat16) for weight in weights], axis=0))
            mixed = mixed * share + acc_ref[block, at] * (fade * share)
            rows = slice(block * BLK, (block + 1) * BLK)
            out_ref[rows, at * HD : (at + 1) * HD] = mixed.T.astype(jnp.bfloat16)


def attend(heads, where_block, counts, queries, past, stats, pieces):
    blocks = queries.shape[0]
    rows = blocks * BLK
    slots = where_block.shape[0] // blocks
    inner = len(heads)
    total_blocks = sum(piece.shape[0] for piece in pieces)

    def of_heads(*shape):
        whole = (pl.Element(blocks), pl.Element(inner), pl.Element(shape[0]), pl.Element(shape[1]))
        return pl.BlockSpec(whole, lambda i, *_: (0, heads[0], 0, 0))

    return call(
        functools.partial(attend_body, blocks, slots, inner),
        (1,),
        [of_heads(HD, BLK), of_heads(HD, BLK), of_heads(2, BLK)]
        + [pl.BlockSpec(memory_space=pl.ANY)] * len(pieces),
        pl.BlockSpec((rows, inner * HD), lambda i, *_: (0, 0)),
        jax.ShapeDtypeStruct((rows, inner * HD), jnp.bfloat16),
        12,
        scratch=[
            pltpu.VMEM((total_blocks, inner, 2, BLK, HD), jnp.bfloat16),
            pltpu.SemaphoreType.DMA((len(pieces),)),
        ],
        prefetch=2,
        micros=ATT_COST,
    )(where_block, counts, queries, past, stats, *pieces)


def part_body(count, state_ref, w_ref, *rest):
    pieces, out_ref = rest[:count], rest[count]
    attended = jnp.concatenate([piece[...] for piece in pieces], axis=1)
    out_ref[...] = (state_ref[...].astype(jnp.float32) + dot(attended, w_ref[...])).astype(out_ref.dtype)


def add_heads(state, w_rows, pieces, out_dtype):
    rows, width = state.shape
    return call(
        functools.partial(part_body, len(pieces)),
        (rows // TILE,),
        [pl.BlockSpec((TILE, width), lambda i: (i, 0)), pl.BlockSpec(w_rows.shape, lambda i: (0, 0))]
        + [pl.BlockSpec((TILE, piece.shape[1]), lambda i: (i, 0)) for piece in pieces],
        pl.BlockSpec((TILE, width), lambda i: (i, 0)),
        jax.ShapeDtypeStruct((rows, width), out_dtype),
        18,
        micros=PART_COST,
    )(state, w_rows, *pieces)


def turn_body(count, part_ref, w_ref, gain_ref, wk_ref, wv_ref, *rest):
    pieces, (state_ref, kv_ref, kv_scr) = rest[:count], rest[count:]

    @pl.when(pl.program_id(0) == 0)
    def _():
        kv_scr[:, :HD] = wk_ref[...]
        kv_scr[:, HD:] = wv_ref[...]

    attended = jnp.concatenate([piece[...] for piece in pieces], axis=1)
    state = (part_ref[...] + dot(attended, w_ref[...])).astype(jnp.bfloat16)
    state_ref[...] = state
    both = dot(normalize(state.astype(jnp.float32), gain_ref[...]), kv_scr[...])
    store_blocks(kv_ref, 0, both[:, :HD], both[:, HD:])


def turn(part, w_rows, pieces, gain, w_key, w_value):
    rows, width = part.shape
    per_tile = TILE // BLK
    tile = pl.BlockSpec((TILE, width), lambda i: (i, 0))
    return call(
        functools.partial(turn_body, len(pieces)),
        (rows // TILE,),
        [
            tile,
            pl.BlockSpec(w_rows.shape, lambda i: (0, 0)),
            pl.BlockSpec((width,), lambda i: (0,)),
            pl.BlockSpec((width, HD), lambda i: (0, 0)),
            pl.BlockSpec((width, HD), lambda i: (0, 0)),
        ]
        + [pl.BlockSpec((TILE, piece.shape[1]), lambda i: (i, 0)) for piece in pieces],
        [tile, pl.BlockSpec((per_tile, 1, 2, BLK, HD), lambda i: (i, 0, 0, 0, 0))],
        [
            jax.ShapeDtypeStruct((rows, width), jnp.bfloat16),
            jax.ShapeDtypeStruct((rows // BLK, 1, 2, BLK, HD), jnp.bfloat16),
        ],
        18,
        scratch=[pltpu.VMEM((width, 2 * HD), jnp.bfloat16)],
        micros=7.0,
    )(part, w_rows, gain, w_key, w_value, *pieces)


def facing(kv):
    half = kv.shape[0] // 2
    return lax.dynamic_slice_in_dim(kv, half * (1 - lax.axis_index("space") % 2), half, 0)


def halo(kv):
    return sent(kv, across), sent(facing(kv), beyond), sent(kv, beside)


def fetch_rows(w_out):
    half = lax.axis_size("space") // 2
    local, width = w_out.shape
    me = lax.axis_index("space")
    quarters = w_out.reshape(local // HD, 4, HD // 4, width)
    mine = lax.dynamic_index_in_dim(quarters, me % 2 + 2 * (me // half), 1, keepdims=False)
    return around(mine, "head")[1:]


def share_rows(w_out, fetched, then):
    fetched = jnp.stack(fetched)
    count = lax.axis_size("space")
    half = count // 2
    local, width = w_out.shape
    heads = local // HD
    me = lax.axis_index("space")
    second = sent(fetched, beside)
    third = sent(fetched, opposite)
    fourth = sent(after(third, then), beside)
    odd, upper = me % 2 == 1, me >= half
    near = (jnp.where(odd, second, fetched), jnp.where(odd, fetched, second))
    far = (jnp.where(odd, fourth, third), jnp.where(odd, third, fourth))
    four = [jnp.where(upper, b, a) for a, b in zip(near + far, far + near, strict=True)]
    others = jnp.stack(four, axis=2).reshape(-1, heads, HD, width)
    return jnp.concatenate([w_out.reshape(1, heads, HD, width), others])


def on_device(snapshot, norm_gain, w_query, w_key, w_value, w_out, cache_key, cache_value, pattern, counts):
    tok_rows, width = snapshot.shape
    blocks = tok_rows // BLK
    half = blocks // 2
    count = blocks * lax.axis_size("space")
    me = lax.axis_index("space")
    own_block = jnp.arange(blocks, dtype=jnp.int32)[:, None]
    relative = (pattern - own_block - me * blocks + count // 2) % count - count // 2
    place = own_block + blocks + half + relative
    turn_by = jnp.where(place < half + blocks, 2 * blocks, jnp.where(place < half + 2 * blocks, 0, -2 * blocks))
    end = 3 * blocks + half
    turn_by = jnp.where(place < half, end, jnp.where(place >= end, -end, turn_by))
    where_block = jnp.where(me % 2 == 1, place + turn_by, place).reshape(-1)
    state = snapshot
    kv_first = first_projection(state, norm_gain, w_key, w_value)
    last = []
    for rollout in range(STEPS):
        near = [halo(kv_first)]
        *kv_rest, queries = rest_projection(state, norm_gain, w_query, w_key, w_value, REST_VMEM[rollout])
        kv = [kv_first] + list(kv_rest)
        near += [halo(piece) for piece in kv_rest]
        if rollout == 0:
            fetched = fetch_rows(w_out)
            queries = after(queries, *fetched[:2])
        past, stats = attend_past(queries, cache_key, cache_value, last)
        came = []
        attended = past
        for chunk, of_chunk in enumerate(CHUNKS):
            next_pair, further, other = near[chunk]
            shared = sent(facing(after(next_pair, attended)), beside)
            own = kv[chunk]
            if chunk == 0 and rollout == 0:
                own = after(own, *fetched)
            if chunk >= 1:
                own = after(own, *came[-1][1:R1PIN])
            if chunk >= 2:
                own = after(own, *came[-2][2:])
            pieces = (further, next_pair, own, other, shared)
            attended = attend(of_chunk, where_block, counts, queries, past, stats, pieces)
            if rollout == 0 and chunk == 0:
                fetched = [after(piece, attended) for piece in fetched]
            came.append(around(attended, "head", came[-1][2:] if came else ()))
        if rollout == 0:
            rows_of = share_rows(w_out, fetched, came[-1][1])
        if rollout == 0:
            w_early = rows_of[:, : CHUNKS[-1][0]].reshape(-1, width)
            w_last = rows_of[:, CHUNKS[-1][0] :].reshape(-1, width)
        early = [piece for group in zip(*came[:-1], strict=True) for piece in group]
        part = add_heads(state, w_early, early, jnp.float32)
        if rollout + 1 < STEPS:
            state, kv_first = turn(part, w_last, came[-1], norm_gain, w_key, w_value)
            last = kv
        else:
            state = add_heads(part, w_last, came[-1], jnp.bfloat16)
    return state


def solution(mesh):
    placed = (
        P("space", None),
        P(),
        P(None, "head"),
        P(None, "head"),
        P(None, "head"),
        P("head", None),
        P(None, "space", "head"),
        P(None, "space", "head"),
        P("space", None),
        P("space"),
    )
    return jax.shard_map(
        on_device, mesh=mesh, in_specs=placed, out_specs=P("space", None), check_vma=False
    )
```

```python
import functools
import math

import jax
import jax.numpy as jnp
from jax import lax
from jax.experimental import pallas as pl
from jax.experimental.pallas import tpu as pltpu
from jax.sharding import PartitionSpec as P

HD = 128
BLK = 128
STEPS = 2
TILE = 256
COST = 3.0
AHEAD = 2
C2PIN = 1
ATT_PINS = (3, 2)
SEND_PIN = 2
ATT_COST = 0.0
PART_COST = 0.0
PAST_VMEM = 49
REST_VMEM = (62, 16)
CHUNKS = ((0,), (1,), (2,))
MIB = 1024 * 1024
SCALE = math.log2(math.e) / math.sqrt(HD)


def sent(value, to):
    count = lax.axis_size("space")
    return lax.ppermute(value, "space", [(i, to(i, count) % count) for i in range(count)])


def across(i, count):
    return i + 1 if i % 2 else i - 1


def beyond(i, count):
    return i - 2 if i % 2 else i + 2


def beside(i, count):
    return i ^ 1


def opposite(i, count):
    return i + count // 2


def turned(value, axis, hops):
    count = lax.axis_size(axis)
    order = list(range(0, count, 2)) + list(range(1, count, 2))[::-1]
    return lax.ppermute(value, axis, [(order[i], order[(i + hops) % count]) for i in range(count)])


def around(value, axis, then=()):
    came = [value]
    for hop in range(1, lax.axis_size(axis)):
        sign = 1 if hop % 2 == 1 else -1
        came.append(turned(came[0] if hop <= 2 else after(came[hop - 2], *then), axis, sign))
    return came


def after(value, *others):
    return lax.optimization_barrier((value,) + others)[0]


def call(body, grid, in_specs, out_specs, out_shape, vmem, scratch=(), prefetch=0, micros=0.0):
    return pl.pallas_call(
        body,
        grid_spec=pltpu.PrefetchScalarGridSpec(
            num_scalar_prefetch=prefetch,
            grid=grid,
            in_specs=in_specs,
            out_specs=out_specs,
            scratch_shapes=list(scratch),
        ),
        out_shape=out_shape,
        compiler_params=pltpu.CompilerParams(
            dimension_semantics=("arbitrary",) * len(grid), vmem_limit_bytes=vmem * MIB
        ),
        cost_estimate=pl.CostEstimate(flops=int(COST * micros * 1.15e9), bytes_accessed=0, transcendentals=0),
    )


def dot(a, b):
    return jnp.dot(a, b, preferred_element_type=jnp.float32)


def normalize(state, gain):
    meansq = jnp.mean(state * state, axis=-1, keepdims=True)
    return (state * lax.rsqrt(meansq + 1e-05) * gain).astype(jnp.bfloat16)


def store_blocks(kv_ref, at, key, value):
    for block in range(key.shape[0] // BLK):
        rows = slice(block * BLK, (block + 1) * BLK)
        kv_ref[block, at, 0] = key[rows].astype(jnp.bfloat16)
        kv_ref[block, at, 1] = value[rows].T.astype(jnp.bfloat16)


def first_body(state_ref, gain_ref, wk_ref, wv_ref, kv_ref, w_scr):
    @pl.when(pl.program_id(0) == 0)
    def _():
        w_scr[:, :HD] = wk_ref[...]
        w_scr[:, HD:] = wv_ref[...]

    both = dot(normalize(state_ref[...].astype(jnp.float32), gain_ref[...]), w_scr[...])
    store_blocks(kv_ref, 0, both[:, :HD], both[:, HD:])


def first_projection(state, gain, w_key, w_value):
    rows, width = state.shape
    per_tile = TILE // BLK
    return call(
        first_body,
        (rows // TILE,),
        [
            pl.BlockSpec((TILE, width), lambda i: (i, 0)),
            pl.BlockSpec((width,), lambda i: (0,)),
            pl.BlockSpec((width, HD), lambda i: (0, 0)),
            pl.BlockSpec((width, HD), lambda i: (0, 0)),
        ],
        pl.BlockSpec((per_tile, 1, 2, BLK, HD), lambda i: (i, 0, 0, 0, 0)),
        jax.ShapeDtypeStruct((rows // BLK, 1, 2, BLK, HD), jnp.bfloat16),
        60,
        scratch=[pltpu.VMEM((width, 2 * HD), jnp.bfloat16)],
        micros=5.0,
    )(state, gain, w_key, w_value)


def rest_body(heads, state_ref, gain_ref, wq_ref, wk_ref, wv_ref, *outs):
    normed = normalize(state_ref[...].astype(jnp.float32), gain_ref[...])
    key = dot(normed, wk_ref[:, HD:])
    value = dot(normed, wv_ref[:, HD:])
    for chunk, kv_ref in zip(CHUNKS[1:], outs, strict=False):
        for at, head in enumerate(chunk):
            cols = slice((head - 1) * HD, head * HD)
            store_blocks(kv_ref, at, key[:, cols], value[:, cols])
    query = dot(normed, wq_ref[...])
    for block in range(TILE // BLK):
        for head in range(heads):
            part = query[block * BLK : (block + 1) * BLK, head * HD : (head + 1) * HD]
            outs[-1][block, head] = part.T.astype(jnp.bfloat16)


def rest_projection(state, gain, w_query, w_key, w_value, vmem):
    rows, width = state.shape
    local = w_query.shape[1]
    heads = local // HD
    per_tile = TILE // BLK
    full = pl.BlockSpec((width, local), lambda i: (0, 0))
    return call(
        functools.partial(rest_body, heads),
        (rows // TILE,),
        [
            pl.BlockSpec((TILE, width), lambda i: (i, 0)),
            pl.BlockSpec((width,), lambda i: (0,)),
            full,
            full,
            full,
        ],
        [pl.BlockSpec((per_tile, len(c), 2, BLK, HD), lambda i: (i, 0, 0, 0, 0)) for c in CHUNKS[1:]]
        + [pl.BlockSpec((per_tile, heads, HD, BLK), lambda i: (i, 0, 0, 0))],
        [jax.ShapeDtypeStruct((rows // BLK, len(c), 2, BLK, HD), jnp.bfloat16) for c in CHUNKS[1:]]
        + [jax.ShapeDtypeStruct((rows // BLK, heads, HD, BLK), jnp.bfloat16)],
        vmem,
        micros=5.0,
    )(state, gain, w_query, w_key, w_value)


def same_token():
    return lax.broadcasted_iota(jnp.int32, (BLK, BLK), 0) == lax.broadcasted_iota(jnp.int32, (BLK, BLK), 1)


def past_body(frames, heads, newer, qt_ref, ck_hbm, cv_hbm, *rest):
    last, (acc_ref, stat_ref, slots, sems) = rest[:-4], rest[-4:]
    place = {head: (c, at) for c, chunk in enumerate(CHUNKS) for at, head in enumerate(chunk)}
    tile = pl.program_id(0)

    def copies(tile):
        rows = pl.ds(pl.multiple_of(tile * TILE, TILE), TILE)
        return [
            pltpu.make_async_copy(cache.at[:, rows], slots.at[tile, which], sems.at[tile, which])
            for which, cache in enumerate((ck_hbm, cv_hbm))
        ]

    @pl.when(tile == 0)
    def _():
        for ahead in range(AHEAD):
            for copy in copies(ahead):
                copy.start()

    @pl.when(tile + AHEAD < pl.num_programs(0))
    def _():
        for copy in copies(tile + AHEAD):
            copy.start()

    for copy in copies(tile):
        copy.wait()
    ck_ref, cv_ref = (slots.at[tile, which] for which in range(2))
    eye = same_token()
    none = jnp.zeros((BLK, BLK), jnp.bfloat16)
    for block in range(qt_ref.shape[0]):
        rows = slice(block * BLK, (block + 1) * BLK)
        for head in range(heads):
            cols = slice(head * HD, (head + 1) * HD)
            keys = [ck_ref[frame, rows, cols] for frame in range(frames)]
            if newer:
                keys[0] = last[place[head][0]][block, place[head][1], 0]
            pairs = dot(jnp.concatenate(keys, axis=0), qt_ref[block, head])
            scores = [
                jnp.sum(jnp.where(eye, pairs[frame * BLK : (frame + 1) * BLK], 0.0), axis=0, keepdims=True)
                for frame in range(frames)
            ]
            top = functools.reduce(jnp.maximum, scores)
            weights = [jnp.exp2((score - top) * SCALE) for score in scores]
            stat_ref[block, head, 0:1] = top
            stat_ref[block, head, 1:2] = functools.reduce(jnp.add, weights)
            spread = [jnp.where(eye, weight, 0.0).astype(jnp.bfloat16) for weight in weights]
            if newer:
                spread[0] = none
            values = jnp.concatenate([cv_ref[frame, rows, cols] for frame in range(frames)], axis=0)
            mixed = dot(jnp.concatenate(spread, axis=1), values).T
            if newer:
                mixed = mixed + last[place[head][0]][block, place[head][1], 1].astype(jnp.float32) * weights[0]
            acc_ref[block, head] = mixed


def attend_past(queries, cache_key, cache_value, last):
    blocks, heads = queries.shape[:2]
    frames, rows, local = cache_key.shape
    per_tile = TILE // BLK
    cached = pl.BlockSpec(memory_space=pltpu.HBM)
    return call(
        functools.partial(past_body, frames, heads, len(last) > 0),
        (blocks // per_tile,),
        [pl.BlockSpec((per_tile, heads, HD, BLK), lambda i: (i, 0, 0, 0)), cached, cached]
        + [pl.BlockSpec((per_tile, *piece.shape[1:]), lambda i: (i, 0, 0, 0, 0)) for piece in last],
        [
            pl.BlockSpec((per_tile, heads, HD, BLK), lambda i: (i, 0, 0, 0)),
            pl.BlockSpec((per_tile, heads, 2, BLK), lambda i: (i, 0, 0, 0)),
        ],
        [
            jax.ShapeDtypeStruct((blocks, heads, HD, BLK), jnp.float32),
            jax.ShapeDtypeStruct((blocks, heads, 2, BLK), jnp.float32),
        ],
        PAST_VMEM,
        scratch=[
            pltpu.VMEM((blocks // per_tile, 2, frames, TILE, local), jnp.bfloat16),
            pltpu.SemaphoreType.DMA((blocks // per_tile, 2)),
        ],
        micros=6.0,
    )(queries, cache_key, cache_value, *last)


def attend_body(blocks, slots, inner, where_ref, counts_ref, qt_ref, acc_ref, stat_ref, *rest):
    pieces, (out_ref, window, sem) = rest[:-3], rest[-3:]
    place = 0
    copies = []
    for piece in pieces:
        copies.append(pltpu.make_async_copy(piece, window.at[pl.ds(place, piece.shape[0])], sem.at[len(copies)]))
        place += piece.shape[0]
    for copy in copies:
        copy.start()
    for copy in copies:
        copy.wait()
    for block in range(blocks):
        live = counts_ref[block]
        places = [where_ref[block * slots + slot] for slot in range(slots)]
        for at in range(inner):
            pairs = dot(jnp.concatenate([window[p, at, 0] for p in places], axis=0), qt_ref[block, at])
            scores = [pairs[:BLK]]
            for slot in range(1, slots):
                score = pairs[slot * BLK : (slot + 1) * BLK]
                scores.append(jnp.where(slot < live, score, jnp.float32(-1e30)))
            past_top = stat_ref[block, at, 0:1]
            top = jnp.maximum(functools.reduce(jnp.maximum, scores).max(axis=0, keepdims=True), past_top)
            weights = [jnp.exp2((score - top) * SCALE) for score in scores]
            fade = jnp.exp2((past_top - top) * SCALE)
            total = functools.reduce(jnp.add, weights).sum(axis=0, keepdims=True) + stat_ref[block, at, 1:2] * fade
            share = 1.0 / total
            values = jnp.concatenate([window[p, at, 1] for p in places], axis=1)
            mixed = dot(values, jnp.concatenate([weight.astype(jnp.bfloat16) for weight in weights], axis=0))
            mixed = mixed * share + acc_ref[block, at] * (fade * share)
            rows = slice(block * BLK, (block + 1) * BLK)
            out_ref[rows, at * HD : (at + 1) * HD] = mixed.T.astype(jnp.bfloat16)


def attend(heads, where_block, counts, queries, past, stats, pieces):
    blocks = queries.shape[0]
    rows = blocks * BLK
    slots = where_block.shape[0] // blocks
    inner = len(heads)
    total_blocks = sum(piece.shape[0] for piece in pieces)

    def of_heads(*shape):
        whole = (pl.Element(blocks), pl.Element(inner), pl.Element(shape[0]), pl.Element(shape[1]))
        return pl.BlockSpec(whole, lambda i, *_: (0, heads[0], 0, 0))

    return call(
        functools.partial(attend_body, blocks, slots, inner),
        (1,),
        [of_heads(HD, BLK), of_heads(HD, BLK), of_heads(2, BLK)]
        + [pl.BlockSpec(memory_space=pl.ANY)] * len(pieces),
        pl.BlockSpec((rows, inner * HD), lambda i, *_: (0, 0)),
        jax.ShapeDtypeStruct((rows, inner * HD), jnp.bfloat16),
        12,
        scratch=[
            pltpu.VMEM((total_blocks, inner, 2, BLK, HD), jnp.bfloat16),
            pltpu.SemaphoreType.DMA((len(pieces),)),
        ],
        prefetch=2,
        micros=ATT_COST,
    )(where_block, counts, queries, past, stats, *pieces)


def part_body(count, state_ref, w_ref, *rest):
    pieces, out_ref = rest[:count], rest[count]
    attended = jnp.concatenate([piece[...] for piece in pieces], axis=1)
    out_ref[...] = (state_ref[...].astype(jnp.float32) + dot(attended, w_ref[...])).astype(out_ref.dtype)


def add_heads(state, w_rows, pieces, out_dtype):
    rows, width = state.shape
    return call(
        functools.partial(part_body, len(pieces)),
        (rows // TILE,),
        [pl.BlockSpec((TILE, width), lambda i: (i, 0)), pl.BlockSpec(w_rows.shape, lambda i: (0, 0))]
        + [pl.BlockSpec((TILE, piece.shape[1]), lambda i: (i, 0)) for piece in pieces],
        pl.BlockSpec((TILE, width), lambda i: (i, 0)),
        jax.ShapeDtypeStruct((rows, width), out_dtype),
        18,
        micros=PART_COST,
    )(state, w_rows, *pieces)


def turn_body(count, part_ref, w_ref, gain_ref, wk_ref, wv_ref, *rest):
    pieces, (state_ref, kv_ref, kv_scr) = rest[:count], rest[count:]

    @pl.when(pl.program_id(0) == 0)
    def _():
        kv_scr[:, :HD] = wk_ref[...]
        kv_scr[:, HD:] = wv_ref[...]

    attended = jnp.concatenate([piece[...] for piece in pieces], axis=1)
    state = (part_ref[...] + dot(attended, w_ref[...])).astype(jnp.bfloat16)
    state_ref[...] = state
    both = dot(normalize(state.astype(jnp.float32), gain_ref[...]), kv_scr[...])
    store_blocks(kv_ref, 0, both[:, :HD], both[:, HD:])


def turn(part, w_rows, pieces, gain, w_key, w_value):
    rows, width = part.shape
    per_tile = TILE // BLK
    tile = pl.BlockSpec((TILE, width), lambda i: (i, 0))
    return call(
        functools.partial(turn_body, len(pieces)),
        (rows // TILE,),
        [
            tile,
            pl.BlockSpec(w_rows.shape, lambda i: (0, 0)),
            pl.BlockSpec((width,), lambda i: (0,)),
            pl.BlockSpec((width, HD), lambda i: (0, 0)),
            pl.BlockSpec((width, HD), lambda i: (0, 0)),
        ]
        + [pl.BlockSpec((TILE, piece.shape[1]), lambda i: (i, 0)) for piece in pieces],
        [tile, pl.BlockSpec((per_tile, 1, 2, BLK, HD), lambda i: (i, 0, 0, 0, 0))],
        [
            jax.ShapeDtypeStruct((rows, width), jnp.bfloat16),
            jax.ShapeDtypeStruct((rows // BLK, 1, 2, BLK, HD), jnp.bfloat16),
        ],
        18,
        scratch=[pltpu.VMEM((width, 2 * HD), jnp.bfloat16)],
        micros=7.0,
    )(part, w_rows, gain, w_key, w_value, *pieces)


def facing(kv):
    half = kv.shape[0] // 2
    return lax.dynamic_slice_in_dim(kv, half * (1 - lax.axis_index("space") % 2), half, 0)


def halo(kv):
    return sent(kv, across), sent(facing(kv), beyond), sent(kv, beside)


def fetch_rows(w_out, then):
    half = lax.axis_size("space") // 2
    local, width = w_out.shape
    me = lax.axis_index("space")
    quarters = w_out.reshape(local // HD, 4, HD // 4, width)
    mine = lax.dynamic_index_in_dim(quarters, me % 2 + 2 * (me // half), 1, keepdims=False)
    return around(after(mine, then), "head")[1:]


def share_rows(w_out, fetched, then):
    fetched = jnp.stack(fetched)
    count = lax.axis_size("space")
    half = count // 2
    local, width = w_out.shape
    heads = local // HD
    me = lax.axis_index("space")
    second = sent(fetched, beside)
    third = sent(fetched, opposite)
    fourth = sent(after(third, then), beside)
    odd, upper = me % 2 == 1, me >= half
    near = (jnp.where(odd, second, fetched), jnp.where(odd, fetched, second))
    far = (jnp.where(odd, fourth, third), jnp.where(odd, third, fourth))
    four = [jnp.where(upper, b, a) for a, b in zip(near + far, far + near, strict=True)]
    others = jnp.stack(four, axis=2).reshape(-1, heads, HD, width)
    return jnp.concatenate([w_out.reshape(1, heads, HD, width), others])


def on_device(snapshot, norm_gain, w_query, w_key, w_value, w_out, cache_key, cache_value, pattern, counts):
    tok_rows, width = snapshot.shape
    blocks = tok_rows // BLK
    half = blocks // 2
    count = blocks * lax.axis_size("space")
    me = lax.axis_index("space")
    own_block = jnp.arange(blocks, dtype=jnp.int32)[:, None]
    relative = (pattern - own_block - me * blocks + count // 2) % count - count // 2
    place = own_block + blocks + half + relative
    turn_by = jnp.where(place < half + blocks, 2 * blocks, jnp.where(place < half + 2 * blocks, 0, -2 * blocks))
    end = 3 * blocks + half
    turn_by = jnp.where(place < half, end, jnp.where(place >= end, -end, turn_by))
    where_block = jnp.where(me % 2 == 1, place + turn_by, place).reshape(-1)
    state = snapshot
    kv_first = first_projection(state, norm_gain, w_key, w_value)
    last = []
    for rollout in range(STEPS):
        near = [halo(kv_first)]
        *kv_rest, queries = rest_projection(state, norm_gain, w_query, w_key, w_value, REST_VMEM[rollout])
        kv = [kv_first] + list(kv_rest)
        near += [halo(piece) for piece in kv_rest]
        if rollout == 0:
            fetched = fetch_rows(w_out, kv_first)
            queries = after(queries, *fetched[:2])
        past, stats = attend_past(queries, cache_key, cache_value, last)
        came = []
        attended = past
        for chunk, of_chunk in enumerate(CHUNKS):
            next_pair, further, other = near[chunk]
            held = (attended, further) if chunk == 0 and rollout >= C2PIN else (attended,)
            shared = sent(facing(after(next_pair, *held)), beside)
            own = kv[chunk]
            if chunk == 0 and rollout == 0:
                own = after(own, *fetched)
            if chunk >= 1:
                own = after(own, *came[-1][1 : ATT_PINS[chunk - 1]])
            pieces = (further, next_pair, own, other, shared)
            attended = attend(of_chunk, where_block, counts, queries, past, stats, pieces)
            if rollout == 0 and chunk == 0:
                fetched = [after(piece, attended) for piece in fetched]
            if 1 <= chunk <= SEND_PIN:
                attended = after(attended, came[-1][-1])
            came.append(around(attended, "head", came[-1][2:] if came else ()))
        if rollout == 0:
            rows_of = share_rows(w_out, fetched, came[-1][1])
        if rollout == 0:
            w_early = rows_of[:, : CHUNKS[-1][0]].reshape(-1, width)
            w_last = rows_of[:, CHUNKS[-1][0] :].reshape(-1, width)
        early = [piece for group in zip(*came[:-1], strict=True) for piece in group]
        part = add_heads(state, w_early, early, jnp.float32)
        if rollout + 1 < STEPS:
            state, kv_first = turn(part, w_last, came[-1], norm_gain, w_key, w_value)
            last = kv
        else:
            state = add_heads(part, w_last, came[-1], jnp.bfloat16)
    return state


def solution(mesh):
    placed = (
        P("space", None),
        P(),
        P(None, "head"),
        P(None, "head"),
        P(None, "head"),
        P("head", None),
        P(None, "space", "head"),
        P(None, "space", "head"),
        P("space", None),
        P("space"),
    )
    return jax.shard_map(
        on_device, mesh=mesh, in_specs=placed, out_specs=P("space", None), check_vma=False
    )
```

```python
import functools
import math

import jax
import jax.numpy as jnp
from jax import lax
from jax.experimental import pallas as pl
from jax.experimental.pallas import tpu as pltpu
from jax.sharding import PartitionSpec as P

HD = 128
BLK = 128
STEPS = 2
TILE = 256
REST_TILE = 512
ADD_TILE = 512
COST = 3.0
AHEAD = 2
C2PIN = 1
WPAST = 0
WPINS = (2, 3)
SENDALL = 2
SHARE = 0
ATT_PINS = (3, 2)
SEND_PIN = 2
ATT_COST = 0.0
PART_COST = 0.0
PAST_VMEM = 49
REST_VMEM = (62, 16)
CHUNKS = ((0,), (1,), (2,))
MIB = 1024 * 1024
SCALE = math.log2(math.e) / math.sqrt(HD)


def sent(value, to):
    count = lax.axis_size("space")
    return lax.ppermute(value, "space", [(i, to(i, count) % count) for i in range(count)])


def across(i, count):
    return i + 1 if i % 2 else i - 1


def beyond(i, count):
    return i - 2 if i % 2 else i + 2


def beside(i, count):
    return i ^ 1


def opposite(i, count):
    return i + count // 2


def turned(value, axis, hops):
    count = lax.axis_size(axis)
    order = list(range(0, count, 2)) + list(range(1, count, 2))[::-1]
    return lax.ppermute(value, axis, [(order[i], order[(i + hops) % count]) for i in range(count)])


def around(value, axis, then=()):
    came = [value]
    for hop in range(1, lax.axis_size(axis)):
        sign = 1 if hop % 2 == 1 else -1
        came.append(turned(came[0] if hop <= 2 else after(came[hop - 2], *then), axis, sign))
    return came


def after(value, *others):
    return lax.optimization_barrier((value,) + others)[0]


def call(body, grid, in_specs, out_specs, out_shape, vmem, scratch=(), prefetch=0, micros=0.0):
    return pl.pallas_call(
        body,
        grid_spec=pltpu.PrefetchScalarGridSpec(
            num_scalar_prefetch=prefetch,
            grid=grid,
            in_specs=in_specs,
            out_specs=out_specs,
            scratch_shapes=list(scratch),
        ),
        out_shape=out_shape,
        compiler_params=pltpu.CompilerParams(
            dimension_semantics=("arbitrary",) * len(grid), vmem_limit_bytes=vmem * MIB
        ),
        cost_estimate=pl.CostEstimate(flops=int(COST * micros * 1.15e9), bytes_accessed=0, transcendentals=0),
    )


def dot(a, b):
    return jnp.dot(a, b, preferred_element_type=jnp.float32)


def normalize(state, gain):
    meansq = jnp.mean(state * state, axis=-1, keepdims=True)
    return (state * lax.rsqrt(meansq + 1e-05) * gain).astype(jnp.bfloat16)


def store_blocks(kv_ref, at, key, value):
    for block in range(key.shape[0] // BLK):
        rows = slice(block * BLK, (block + 1) * BLK)
        kv_ref[block, at, 0] = key[rows].astype(jnp.bfloat16)
        kv_ref[block, at, 1] = value[rows].T.astype(jnp.bfloat16)


def position():
    me, count = lax.axis_index("space"), lax.axis_size("space")
    return lax.rem(me, 2), lax.rem(me, 2) + 2 * lax.div(me, count // 2)


def store_first(kv_ref, facing_ref, both):
    store_blocks(kv_ref, 0, both[:, :HD], both[:, HD:])

    @pl.when(pl.program_id(0) == 1 - position()[0])
    def _():
        store_blocks(facing_ref, 0, both[:, :HD], both[:, HD:])


def first_body(state_ref, gain_ref, wk_ref, wv_ref, w_out_hbm, kv_ref, facing_ref, mine_ref, w_scr, sems):
    heads, slice_rows, _ = mine_ref.shape
    copies = []
    for head in range(heads):
        rows = pl.ds(pl.multiple_of(head * HD + position()[1] * slice_rows, slice_rows), slice_rows)
        copies.append(pltpu.make_async_copy(w_out_hbm.at[rows], mine_ref.at[head], sems.at[head]))

    @pl.when(pl.program_id(0) == 0)
    def _():
        for copy in copies:
            copy.start()
        w_scr[:, :HD] = wk_ref[...]
        w_scr[:, HD:] = wv_ref[...]

    store_first(kv_ref, facing_ref, dot(normalize(state_ref[...].astype(jnp.float32), gain_ref[...]), w_scr[...]))

    @pl.when(pl.program_id(0) == pl.num_programs(0) - 1)
    def _():
        for copy in copies:
            copy.wait()


def first_projection(state, gain, w_key, w_value, w_out):
    rows, width = state.shape
    half = rows // 2
    heads = w_out.shape[0] // HD
    return call(
        first_body,
        (2,),
        [
            pl.BlockSpec((half, width), lambda i: (i, 0)),
            pl.BlockSpec((width,), lambda i: (0,)),
            pl.BlockSpec((width, HD), lambda i: (0, 0)),
            pl.BlockSpec((width, HD), lambda i: (0, 0)),
            pl.BlockSpec(memory_space=pltpu.HBM),
        ],
        [
            pl.BlockSpec((half // BLK, 1, 2, BLK, HD), lambda i: (i, 0, 0, 0, 0)),
            pl.BlockSpec((half // BLK, 1, 2, BLK, HD), lambda i: (0, 0, 0, 0, 0)),
            pl.BlockSpec((heads, HD // 4, width), lambda i: (0, 0, 0)),
        ],
        [
            jax.ShapeDtypeStruct((rows // BLK, 1, 2, BLK, HD), jnp.bfloat16),
            jax.ShapeDtypeStruct((half // BLK, 1, 2, BLK, HD), jnp.bfloat16),
            jax.ShapeDtypeStruct((heads, HD // 4, width), jnp.bfloat16),
        ],
        60,
        scratch=[pltpu.VMEM((width, 2 * HD), jnp.bfloat16), pltpu.SemaphoreType.DMA((heads,))],
        micros=5.0,
    )(state, gain, w_key, w_value, w_out)


def rest_body(heads, state_ref, gain_ref, wq_ref, wk_ref, wv_ref, *outs):
    normed = normalize(state_ref[...].astype(jnp.float32), gain_ref[...])
    key = dot(normed, wk_ref[:, HD:])
    value = dot(normed, wv_ref[:, HD:])
    for chunk, kv_ref in zip(CHUNKS[1:], outs, strict=False):
        for at, head in enumerate(chunk):
            cols = slice((head - 1) * HD, head * HD)
            store_blocks(kv_ref, at, key[:, cols], value[:, cols])
    query = dot(normed, wq_ref[...])
    for block in range(REST_TILE // BLK):
        for head in range(heads):
            part = query[block * BLK : (block + 1) * BLK, head * HD : (head + 1) * HD]
            outs[-1][block, head] = part.T.astype(jnp.bfloat16)


def rest_projection(state, gain, w_query, w_key, w_value, vmem):
    rows, width = state.shape
    local = w_query.shape[1]
    heads = local // HD
    per_tile = REST_TILE // BLK
    full = pl.BlockSpec((width, local), lambda i: (0, 0))
    return call(
        functools.partial(rest_body, heads),
        (rows // REST_TILE,),
        [
            pl.BlockSpec((REST_TILE, width), lambda i: (i, 0)),
            pl.BlockSpec((width,), lambda i: (0,)),
            full,
            full,
            full,
        ],
        [pl.BlockSpec((per_tile, len(c), 2, BLK, HD), lambda i: (i, 0, 0, 0, 0)) for c in CHUNKS[1:]]
        + [pl.BlockSpec((per_tile, heads, HD, BLK), lambda i: (i, 0, 0, 0))],
        [jax.ShapeDtypeStruct((rows // BLK, len(c), 2, BLK, HD), jnp.bfloat16) for c in CHUNKS[1:]]
        + [jax.ShapeDtypeStruct((rows // BLK, heads, HD, BLK), jnp.bfloat16)],
        vmem,
        micros=5.0,
    )(state, gain, w_query, w_key, w_value)


def same_token():
    return lax.broadcasted_iota(jnp.int32, (BLK, BLK), 0) == lax.broadcasted_iota(jnp.int32, (BLK, BLK), 1)


def past_body(frames, heads, newer, qt_ref, ck_hbm, cv_hbm, *rest):
    last, (acc_ref, stat_ref, slots, sems) = rest[:-4], rest[-4:]
    place = {head: (c, at) for c, chunk in enumerate(CHUNKS) for at, head in enumerate(chunk)}
    tile = pl.program_id(0)

    def copies(tile):
        rows = pl.ds(pl.multiple_of(tile * TILE, TILE), TILE)
        return [
            pltpu.make_async_copy(cache.at[:, rows], slots.at[tile, which], sems.at[tile, which])
            for which, cache in enumerate((ck_hbm, cv_hbm))
        ]

    @pl.when(tile == 0)
    def _():
        for ahead in range(AHEAD):
            for copy in copies(ahead):
                copy.start()

    @pl.when(tile + AHEAD < pl.num_programs(0))
    def _():
        for copy in copies(tile + AHEAD):
            copy.start()

    for copy in copies(tile):
        copy.wait()
    ck_ref, cv_ref = (slots.at[tile, which] for which in range(2))
    eye = same_token()
    none = jnp.zeros((BLK, BLK), jnp.bfloat16)
    for block in range(qt_ref.shape[0]):
        rows = slice(block * BLK, (block + 1) * BLK)
        for head in range(heads):
            cols = slice(head * HD, (head + 1) * HD)
            keys = [ck_ref[frame, rows, cols] for frame in range(frames)]
            if newer:
                keys[0] = last[place[head][0]][block, place[head][1], 0]
            pairs = dot(jnp.concatenate(keys, axis=0), qt_ref[block, head])
            scores = [
                jnp.sum(jnp.where(eye, pairs[frame * BLK : (frame + 1) * BLK], 0.0), axis=0, keepdims=True)
                for frame in range(frames)
            ]
            top = functools.reduce(jnp.maximum, scores)
            weights = [jnp.exp2((score - top) * SCALE) for score in scores]
            stat_ref[block, head, 0:1] = top
            stat_ref[block, head, 1:2] = functools.reduce(jnp.add, weights)
            spread = [jnp.where(eye, weight, 0.0).astype(jnp.bfloat16) for weight in weights]
            if newer:
                spread[0] = none
            values = jnp.concatenate([cv_ref[frame, rows, cols] for frame in range(frames)], axis=0)
            mixed = dot(jnp.concatenate(spread, axis=1), values).T
            if newer:
                mixed = mixed + last[place[head][0]][block, place[head][1], 1].astype(jnp.float32) * weights[0]
            acc_ref[block, head] = mixed


def attend_past(queries, cache_key, cache_value, last):
    blocks, heads = queries.shape[:2]
    frames, rows, local = cache_key.shape
    per_tile = TILE // BLK
    cached = pl.BlockSpec(memory_space=pltpu.HBM)
    return call(
        functools.partial(past_body, frames, heads, len(last) > 0),
        (blocks // per_tile,),
        [pl.BlockSpec((per_tile, heads, HD, BLK), lambda i: (i, 0, 0, 0)), cached, cached]
        + [pl.BlockSpec((per_tile, *piece.shape[1:]), lambda i: (i, 0, 0, 0, 0)) for piece in last],
        [
            pl.BlockSpec((per_tile, heads, HD, BLK), lambda i: (i, 0, 0, 0)),
            pl.BlockSpec((per_tile, heads, 2, BLK), lambda i: (i, 0, 0, 0)),
        ],
        [
            jax.ShapeDtypeStruct((blocks, heads, HD, BLK), jnp.float32),
            jax.ShapeDtypeStruct((blocks, heads, 2, BLK), jnp.float32),
        ],
        PAST_VMEM,
        scratch=[
            pltpu.VMEM((blocks // per_tile, 2, frames, TILE, local), jnp.bfloat16),
            pltpu.SemaphoreType.DMA((blocks // per_tile, 2)),
        ],
        micros=6.0,
    )(queries, cache_key, cache_value, *last)


def attend_body(blocks, slots, inner, where_ref, counts_ref, qt_ref, acc_ref, stat_ref, *rest):
    pieces, (out_ref, window, sem) = rest[:-3], rest[-3:]
    place = 0
    copies = []
    for piece in pieces:
        copies.append(pltpu.make_async_copy(piece, window.at[pl.ds(place, piece.shape[0])], sem.at[len(copies)]))
        place += piece.shape[0]
    for copy in copies:
        copy.start()
    for copy in copies:
        copy.wait()
    for block in range(blocks):
        live = counts_ref[block]
        places = [where_ref[block * slots + slot] for slot in range(slots)]
        for at in range(inner):
            pairs = dot(jnp.concatenate([window[p, at, 0] for p in places], axis=0), qt_ref[block, at])
            scores = [pairs[:BLK]]
            for slot in range(1, slots):
                score = pairs[slot * BLK : (slot + 1) * BLK]
                scores.append(jnp.where(slot < live, score, jnp.float32(-1e30)))
            past_top = stat_ref[block, at, 0:1]
            top = jnp.maximum(functools.reduce(jnp.maximum, scores).max(axis=0, keepdims=True), past_top)
            weights = [jnp.exp2((score - top) * SCALE) for score in scores]
            fade = jnp.exp2((past_top - top) * SCALE)
            total = functools.reduce(jnp.add, weights).sum(axis=0, keepdims=True) + stat_ref[block, at, 1:2] * fade
            share = 1.0 / total
            values = jnp.concatenate([window[p, at, 1] for p in places], axis=1)
            mixed = dot(values, jnp.concatenate([weight.astype(jnp.bfloat16) for weight in weights], axis=0))
            mixed = mixed * share + acc_ref[block, at] * (fade * share)
            rows = slice(block * BLK, (block + 1) * BLK)
            out_ref[rows, at * HD : (at + 1) * HD] = mixed.T.astype(jnp.bfloat16)


def attend(heads, where_block, counts, queries, past, stats, pieces):
    blocks = queries.shape[0]
    rows = blocks * BLK
    slots = where_block.shape[0] // blocks
    inner = len(heads)
    total_blocks = sum(piece.shape[0] for piece in pieces)

    def of_heads(*shape):
        whole = (pl.Element(blocks), pl.Element(inner), pl.Element(shape[0]), pl.Element(shape[1]))
        return pl.BlockSpec(whole, lambda i, *_: (0, heads[0], 0, 0))

    return call(
        functools.partial(attend_body, blocks, slots, inner),
        (1,),
        [of_heads(HD, BLK), of_heads(HD, BLK), of_heads(2, BLK)]
        + [pl.BlockSpec(memory_space=pl.ANY)] * len(pieces),
        pl.BlockSpec((rows, inner * HD), lambda i, *_: (0, 0)),
        jax.ShapeDtypeStruct((rows, inner * HD), jnp.bfloat16),
        12,
        scratch=[
            pltpu.VMEM((total_blocks, inner, 2, BLK, HD), jnp.bfloat16),
            pltpu.SemaphoreType.DMA((len(pieces),)),
        ],
        prefetch=2,
        micros=ATT_COST,
    )(where_block, counts, queries, past, stats, *pieces)


def part_body(count, state_ref, w_ref, *rest):
    pieces, out_ref = rest[:count], rest[count]
    attended = jnp.concatenate([piece[...] for piece in pieces], axis=1)
    out_ref[...] = (state_ref[...].astype(jnp.float32) + dot(attended, w_ref[...])).astype(out_ref.dtype)


def add_heads(state, w_rows, pieces, out_dtype):
    rows, width = state.shape
    return call(
        functools.partial(part_body, len(pieces)),
        (rows // ADD_TILE,),
        [pl.BlockSpec((ADD_TILE, width), lambda i: (i, 0)), pl.BlockSpec(w_rows.shape, lambda i: (0, 0))]
        + [pl.BlockSpec((ADD_TILE, piece.shape[1]), lambda i: (i, 0)) for piece in pieces],
        pl.BlockSpec((ADD_TILE, width), lambda i: (i, 0)),
        jax.ShapeDtypeStruct((rows, width), out_dtype),
        18,
        micros=PART_COST,
    )(state, w_rows, *pieces)


def turn_body(count, part_ref, w_ref, gain_ref, wk_ref, wv_ref, *rest):
    pieces, (state_ref, kv_ref, facing_ref, kv_scr) = rest[:count], rest[count:]

    @pl.when(pl.program_id(0) == 0)
    def _():
        kv_scr[:, :HD] = wk_ref[...]
        kv_scr[:, HD:] = wv_ref[...]

    attended = jnp.concatenate([piece[...] for piece in pieces], axis=1)
    state = (part_ref[...] + dot(attended, w_ref[...])).astype(jnp.bfloat16)
    state_ref[...] = state
    store_first(kv_ref, facing_ref, dot(normalize(state.astype(jnp.float32), gain_ref[...]), kv_scr[...]))


def turn(part, w_rows, pieces, gain, w_key, w_value):
    rows, width = part.shape
    half = rows // 2
    tile = pl.BlockSpec((half, width), lambda i: (i, 0))
    return call(
        functools.partial(turn_body, len(pieces)),
        (2,),
        [
            tile,
            pl.BlockSpec(w_rows.shape, lambda i: (0, 0)),
            pl.BlockSpec((width,), lambda i: (0,)),
            pl.BlockSpec((width, HD), lambda i: (0, 0)),
            pl.BlockSpec((width, HD), lambda i: (0, 0)),
        ]
        + [pl.BlockSpec((half, piece.shape[1]), lambda i: (i, 0)) for piece in pieces],
        [
            tile,
            pl.BlockSpec((half // BLK, 1, 2, BLK, HD), lambda i: (i, 0, 0, 0, 0)),
            pl.BlockSpec((half // BLK, 1, 2, BLK, HD), lambda i: (0, 0, 0, 0, 0)),
        ],
        [
            jax.ShapeDtypeStruct((rows, width), jnp.bfloat16),
            jax.ShapeDtypeStruct((rows // BLK, 1, 2, BLK, HD), jnp.bfloat16),
            jax.ShapeDtypeStruct((half // BLK, 1, 2, BLK, HD), jnp.bfloat16),
        ],
        18,
        scratch=[pltpu.VMEM((width, 2 * HD), jnp.bfloat16)],
        micros=7.0,
    )(part, w_rows, gain, w_key, w_value, *pieces)


def facing(kv):
    half = kv.shape[0] // 2
    return lax.dynamic_slice_in_dim(kv, half * (1 - lax.axis_index("space") % 2), half, 0)


def halo(kv, faces=None):
    faces = facing(kv) if faces is None else faces
    return sent(kv, across), sent(faces, beyond), sent(kv, beside)


def share_rows(w_out, fetched, then):
    fetched = jnp.stack(fetched)
    count = lax.axis_size("space")
    half = count // 2
    local, width = w_out.shape
    heads = local // HD
    me = lax.axis_index("space")
    second = sent(fetched, beside)
    third = sent(fetched, opposite)
    fourth = sent(after(third, then), beside)
    odd, upper = me % 2 == 1, me >= half
    near = (jnp.where(odd, second, fetched), jnp.where(odd, fetched, second))
    far = (jnp.where(odd, fourth, third), jnp.where(odd, third, fourth))
    four = [jnp.where(upper, b, a) for a, b in zip(near + far, far + near, strict=True)]
    others = jnp.stack(four, axis=2).reshape(-1, heads, HD, width)
    return jnp.concatenate([w_out.reshape(1, heads, HD, width), others])


def on_device(snapshot, norm_gain, w_query, w_key, w_value, w_out, cache_key, cache_value, pattern, counts):
    tok_rows, width = snapshot.shape
    blocks = tok_rows // BLK
    half = blocks // 2
    count = blocks * lax.axis_size("space")
    me = lax.axis_index("space")
    own_block = jnp.arange(blocks, dtype=jnp.int32)[:, None]
    relative = (pattern - own_block - me * blocks + count // 2) % count - count // 2
    place = own_block + blocks + half + relative
    turn_by = jnp.where(place < half + blocks, 2 * blocks, jnp.where(place < half + 2 * blocks, 0, -2 * blocks))
    end = 3 * blocks + half
    turn_by = jnp.where(place < half, end, jnp.where(place >= end, -end, turn_by))
    where_block = jnp.where(me % 2 == 1, place + turn_by, place).reshape(-1)
    state = snapshot
    kv_first, faces, mine = first_projection(state, norm_gain, w_key, w_value, w_out)
    last = []
    for rollout in range(STEPS):
        near = [halo(kv_first, faces)]
        *kv_rest, queries = rest_projection(state, norm_gain, w_query, w_key, w_value, REST_VMEM[rollout])
        kv = [kv_first] + list(kv_rest)
        near += [halo(piece) for piece in kv_rest]
        if rollout == 0:
            fetched = around(mine, "head")[1:]
            queries = after(queries, *fetched[:WPAST])
        past, stats = attend_past(queries, cache_key, cache_value, last)
        came = []
        attended = past
        for chunk, of_chunk in enumerate(CHUNKS):
            next_pair, further, other = near[chunk]
            held = (attended, further) if chunk == 0 and rollout >= C2PIN else (attended,)
            shared = sent(facing(after(next_pair, *held)), beside)
            own = kv[chunk]
            if chunk < 2 and rollout == 0:
                own = after(own, *fetched[: WPINS[chunk]])
            if chunk >= 1:
                own = after(own, *came[-1][1 : ATT_PINS[chunk - 1]])
            pieces = (further, next_pair, own, other, shared)
            attended = attend(of_chunk, where_block, counts, queries, past, stats, pieces)
            if rollout == 0 and chunk == SHARE:
                fetched = [after(piece, attended) for piece in fetched]
            if 1 <= chunk <= SEND_PIN:
                attended = after(attended, *came[-1][SENDALL:])
            came.append(around(attended, "head", came[-1][2:] if came else ()))
        if rollout == 0:
            rows_of = share_rows(w_out, fetched, came[-1][1])
        if rollout == 0:
            w_early = rows_of[:, : CHUNKS[-1][0]].reshape(-1, width)
            w_last = rows_of[:, CHUNKS[-1][0] :].reshape(-1, width)
        early = [piece for group in zip(*came[:-1], strict=True) for piece in group]
        part = add_heads(state, w_early, early, jnp.float32)
        if rollout + 1 < STEPS:
            state, kv_first, faces = turn(part, w_last, came[-1], norm_gain, w_key, w_value)
            last = kv
        else:
            state = add_heads(part, w_last, came[-1], jnp.bfloat16)
    return state


def solution(mesh):
    placed = (
        P("space", None),
        P(),
        P(None, "head"),
        P(None, "head"),
        P(None, "head"),
        P("head", None),
        P(None, "space", "head"),
        P(None, "space", "head"),
        P("space", None),
        P("space"),
    )
    return jax.shard_map(
        on_device, mesh=mesh, in_specs=placed, out_specs=P("space", None), check_vma=False
    )
```

```python
import functools
import math

import jax
import jax.numpy as jnp
from jax import lax
from jax.experimental import pallas as pl
from jax.experimental.pallas import tpu as pltpu
from jax.sharding import PartitionSpec as P

HD = 128
BLK = 128
STEPS = 2
TILE = 256
REST_TILE = 512
ADD_TILE = 512
COST = 3.0
AHEAD = 2
C2PIN = 1
WPAST = 0
WPINS = (2, 3)
SENDALL = 2
SHARE = 0
ATT_PINS = (3, 1)
SEND_PIN = 2
ATT_COST = 0.0
PART_COST = 0.0
PAST_VMEM = 49
REST_VMEM = (62, 16)
CHUNKS = ((0,), (1,), (2,))
MIB = 1024 * 1024
SCALE = math.log2(math.e) / math.sqrt(HD)


def sent(value, to):
    count = lax.axis_size("space")
    return lax.ppermute(value, "space", [(i, to(i, count) % count) for i in range(count)])


def across(i, count):
    return i + 1 if i % 2 else i - 1


def beyond(i, count):
    return i - 2 if i % 2 else i + 2


def beside(i, count):
    return i ^ 1


def opposite(i, count):
    return i + count // 2


def turned(value, axis, hops):
    count = lax.axis_size(axis)
    order = list(range(0, count, 2)) + list(range(1, count, 2))[::-1]
    return lax.ppermute(value, axis, [(order[i], order[(i + hops) % count]) for i in range(count)])


def around(value, axis, then=()):
    came = [value]
    for hop in range(1, lax.axis_size(axis)):
        sign = 1 if hop % 2 == 1 else -1
        came.append(turned(came[0] if hop <= 2 else after(came[hop - 2], *then), axis, sign))
    return came


def after(value, *others):
    return lax.optimization_barrier((value,) + others)[0]


def call(body, grid, in_specs, out_specs, out_shape, vmem, scratch=(), prefetch=0, micros=0.0):
    return pl.pallas_call(
        body,
        grid_spec=pltpu.PrefetchScalarGridSpec(
            num_scalar_prefetch=prefetch,
            grid=grid,
            in_specs=in_specs,
            out_specs=out_specs,
            scratch_shapes=list(scratch),
        ),
        out_shape=out_shape,
        compiler_params=pltpu.CompilerParams(
            dimension_semantics=("arbitrary",) * len(grid), vmem_limit_bytes=vmem * MIB
        ),
        cost_estimate=pl.CostEstimate(flops=int(COST * micros * 1.15e9), bytes_accessed=0, transcendentals=0),
    )


def dot(a, b):
    return jnp.dot(a, b, preferred_element_type=jnp.float32)


def normalize(state, gain):
    meansq = jnp.mean(state * state, axis=-1, keepdims=True)
    return (state * lax.rsqrt(meansq + 1e-05) * gain).astype(jnp.bfloat16)


def store_blocks(kv_ref, at, key, value):
    for block in range(key.shape[0] // BLK):
        rows = slice(block * BLK, (block + 1) * BLK)
        kv_ref[block, at, 0] = key[rows].astype(jnp.bfloat16)
        kv_ref[block, at, 1] = value[rows].T.astype(jnp.bfloat16)


def position():
    me, count = lax.axis_index("space"), lax.axis_size("space")
    return lax.rem(me, 2), lax.rem(me, 2) + 2 * lax.div(me, count // 2)


def store_first(kv_ref, facing_ref, both):
    store_blocks(kv_ref, 0, both[:, :HD], both[:, HD:])

    @pl.when(pl.program_id(0) == 1 - position()[0])
    def _():
        store_blocks(facing_ref, 0, both[:, :HD], both[:, HD:])


def first_body(state_ref, gain_ref, wk_ref, wv_ref, w_out_hbm, kv_ref, facing_ref, mine_ref, w_scr, sems):
    heads, slice_rows, _ = mine_ref.shape
    copies = []
    for head in range(heads):
        rows = pl.ds(pl.multiple_of(head * HD + position()[1] * slice_rows, slice_rows), slice_rows)
        copies.append(pltpu.make_async_copy(w_out_hbm.at[rows], mine_ref.at[head], sems.at[head]))

    @pl.when(pl.program_id(0) == 0)
    def _():
        for copy in copies:
            copy.start()
        w_scr[:, :HD] = wk_ref[...]
        w_scr[:, HD:] = wv_ref[...]

    store_first(kv_ref, facing_ref, dot(normalize(state_ref[...].astype(jnp.float32), gain_ref[...]), w_scr[...]))

    @pl.when(pl.program_id(0) == pl.num_programs(0) - 1)
    def _():
        for copy in copies:
            copy.wait()


def first_projection(state, gain, w_key, w_value, w_out):
    rows, width = state.shape
    half = rows // 2
    heads = w_out.shape[0] // HD
    return call(
        first_body,
        (2,),
        [
            pl.BlockSpec((half, width), lambda i: (i, 0)),
            pl.BlockSpec((width,), lambda i: (0,)),
            pl.BlockSpec((width, HD), lambda i: (0, 0)),
            pl.BlockSpec((width, HD), lambda i: (0, 0)),
            pl.BlockSpec(memory_space=pltpu.HBM),
        ],
        [
            pl.BlockSpec((half // BLK, 1, 2, BLK, HD), lambda i: (i, 0, 0, 0, 0)),
            pl.BlockSpec((half // BLK, 1, 2, BLK, HD), lambda i: (0, 0, 0, 0, 0)),
            pl.BlockSpec((heads, HD // 4, width), lambda i: (0, 0, 0)),
        ],
        [
            jax.ShapeDtypeStruct((rows // BLK, 1, 2, BLK, HD), jnp.bfloat16),
            jax.ShapeDtypeStruct((half // BLK, 1, 2, BLK, HD), jnp.bfloat16),
            jax.ShapeDtypeStruct((heads, HD // 4, width), jnp.bfloat16),
        ],
        60,
        scratch=[pltpu.VMEM((width, 2 * HD), jnp.bfloat16), pltpu.SemaphoreType.DMA((heads,))],
        micros=5.0,
    )(state, gain, w_key, w_value, w_out)


def rest_body(heads, state_ref, gain_ref, wq_ref, wk_ref, wv_ref, *outs):
    normed = normalize(state_ref[...].astype(jnp.float32), gain_ref[...])
    key = dot(normed, wk_ref[:, HD:])
    value = dot(normed, wv_ref[:, HD:])
    for chunk, kv_ref in zip(CHUNKS[1:], outs, strict=False):
        for at, head in enumerate(chunk):
            cols = slice((head - 1) * HD, head * HD)
            store_blocks(kv_ref, at, key[:, cols], value[:, cols])
    query = dot(normed, wq_ref[...])
    for block in range(REST_TILE // BLK):
        for head in range(heads):
            part = query[block * BLK : (block + 1) * BLK, head * HD : (head + 1) * HD]
            outs[-1][block, head] = part.T.astype(jnp.bfloat16)


def rest_projection(state, gain, w_query, w_key, w_value, vmem):
    rows, width = state.shape
    local = w_query.shape[1]
    heads = local // HD
    per_tile = REST_TILE // BLK
    full = pl.BlockSpec((width, local), lambda i: (0, 0))
    return call(
        functools.partial(rest_body, heads),
        (rows // REST_TILE,),
        [
            pl.BlockSpec((REST_TILE, width), lambda i: (i, 0)),
            pl.BlockSpec((width,), lambda i: (0,)),
            full,
            full,
            full,
        ],
        [pl.BlockSpec((per_tile, len(c), 2, BLK, HD), lambda i: (i, 0, 0, 0, 0)) for c in CHUNKS[1:]]
        + [pl.BlockSpec((per_tile, heads, HD, BLK), lambda i: (i, 0, 0, 0))],
        [jax.ShapeDtypeStruct((rows // BLK, len(c), 2, BLK, HD), jnp.bfloat16) for c in CHUNKS[1:]]
        + [jax.ShapeDtypeStruct((rows // BLK, heads, HD, BLK), jnp.bfloat16)],
        vmem,
        micros=5.0,
    )(state, gain, w_query, w_key, w_value)


def same_token():
    return lax.broadcasted_iota(jnp.int32, (BLK, BLK), 0) == lax.broadcasted_iota(jnp.int32, (BLK, BLK), 1)


def past_body(frames, heads, newer, qt_ref, ck_hbm, cv_hbm, *rest):
    last, (acc_ref, stat_ref, slots, sems) = rest[:-4], rest[-4:]
    place = {head: (c, at) for c, chunk in enumerate(CHUNKS) for at, head in enumerate(chunk)}
    tile = pl.program_id(0)

    def copies(tile):
        rows = pl.ds(pl.multiple_of(tile * TILE, TILE), TILE)
        return [
            pltpu.make_async_copy(cache.at[:, rows], slots.at[tile, which], sems.at[tile, which])
            for which, cache in enumerate((ck_hbm, cv_hbm))
        ]

    @pl.when(tile == 0)
    def _():
        for ahead in range(AHEAD):
            for copy in copies(ahead):
                copy.start()

    @pl.when(tile + AHEAD < pl.num_programs(0))
    def _():
        for copy in copies(tile + AHEAD):
            copy.start()

    for copy in copies(tile):
        copy.wait()
    ck_ref, cv_ref = (slots.at[tile, which] for which in range(2))
    eye = same_token()
    none = jnp.zeros((BLK, BLK), jnp.bfloat16)
    for block in range(qt_ref.shape[0]):
        rows = slice(block * BLK, (block + 1) * BLK)
        for head in range(heads):
            cols = slice(head * HD, (head + 1) * HD)
            keys = [ck_ref[frame, rows, cols] for frame in range(frames)]
            if newer:
                keys[0] = last[place[head][0]][block, place[head][1], 0]
            pairs = dot(jnp.concatenate(keys, axis=0), qt_ref[block, head])
            scores = [
                jnp.sum(jnp.where(eye, pairs[frame * BLK : (frame + 1) * BLK], 0.0), axis=0, keepdims=True)
                for frame in range(frames)
            ]
            top = functools.reduce(jnp.maximum, scores)
            weights = [jnp.exp2((score - top) * SCALE) for score in scores]
            stat_ref[block, head, 0:1] = top
            stat_ref[block, head, 1:2] = functools.reduce(jnp.add, weights)
            spread = [jnp.where(eye, weight, 0.0).astype(jnp.bfloat16) for weight in weights]
            if newer:
                spread[0] = none
            values = jnp.concatenate([cv_ref[frame, rows, cols] for frame in range(frames)], axis=0)
            mixed = dot(jnp.concatenate(spread, axis=1), values).T
            if newer:
                mixed = mixed + last[place[head][0]][block, place[head][1], 1].astype(jnp.float32) * weights[0]
            acc_ref[block, head] = mixed


def attend_past(queries, cache_key, cache_value, last):
    blocks, heads = queries.shape[:2]
    frames, rows, local = cache_key.shape
    per_tile = TILE // BLK
    cached = pl.BlockSpec(memory_space=pltpu.HBM)
    return call(
        functools.partial(past_body, frames, heads, len(last) > 0),
        (blocks // per_tile,),
        [pl.BlockSpec((per_tile, heads, HD, BLK), lambda i: (i, 0, 0, 0)), cached, cached]
        + [pl.BlockSpec((per_tile, *piece.shape[1:]), lambda i: (i, 0, 0, 0, 0)) for piece in last],
        [
            pl.BlockSpec((per_tile, heads, HD, BLK), lambda i: (i, 0, 0, 0)),
            pl.BlockSpec((per_tile, heads, 2, BLK), lambda i: (i, 0, 0, 0)),
        ],
        [
            jax.ShapeDtypeStruct((blocks, heads, HD, BLK), jnp.float32),
            jax.ShapeDtypeStruct((blocks, heads, 2, BLK), jnp.float32),
        ],
        PAST_VMEM,
        scratch=[
            pltpu.VMEM((blocks // per_tile, 2, frames, TILE, local), jnp.bfloat16),
            pltpu.SemaphoreType.DMA((blocks // per_tile, 2)),
        ],
        micros=6.0,
    )(queries, cache_key, cache_value, *last)


def attend_body(blocks, slots, inner, where_ref, counts_ref, qt_ref, acc_ref, stat_ref, *rest):
    pieces, (out_ref, window, sem) = rest[:-3], rest[-3:]
    place = 0
    copies = []
    for piece in pieces:
        copies.append(pltpu.make_async_copy(piece, window.at[pl.ds(place, piece.shape[0])], sem.at[len(copies)]))
        place += piece.shape[0]
    for copy in copies:
        copy.start()
    for copy in copies:
        copy.wait()
    for block in range(blocks):
        live = counts_ref[block]
        places = [where_ref[block * slots + slot] for slot in range(slots)]
        for at in range(inner):
            pairs = dot(jnp.concatenate([window[p, at, 0] for p in places], axis=0), qt_ref[block, at])
            scores = [pairs[:BLK]]
            for slot in range(1, slots):
                score = pairs[slot * BLK : (slot + 1) * BLK]
                scores.append(jnp.where(slot < live, score, jnp.float32(-1e30)))
            past_top = stat_ref[block, at, 0:1]
            top = jnp.maximum(functools.reduce(jnp.maximum, scores).max(axis=0, keepdims=True), past_top)
            weights = [jnp.exp2((score - top) * SCALE) for score in scores]
            fade = jnp.exp2((past_top - top) * SCALE)
            total = functools.reduce(jnp.add, weights).sum(axis=0, keepdims=True) + stat_ref[block, at, 1:2] * fade
            share = 1.0 / total
            values = jnp.concatenate([window[p, at, 1] for p in places], axis=1)
            mixed = dot(values, jnp.concatenate([weight.astype(jnp.bfloat16) for weight in weights], axis=0))
            mixed = mixed * share + acc_ref[block, at] * (fade * share)
            rows = slice(block * BLK, (block + 1) * BLK)
            out_ref[rows, at * HD : (at + 1) * HD] = mixed.T.astype(jnp.bfloat16)


def attend(heads, where_block, counts, queries, past, stats, pieces):
    blocks = queries.shape[0]
    rows = blocks * BLK
    slots = where_block.shape[0] // blocks
    inner = len(heads)
    total_blocks = sum(piece.shape[0] for piece in pieces)

    def of_heads(*shape):
        whole = (pl.Element(blocks), pl.Element(inner), pl.Element(shape[0]), pl.Element(shape[1]))
        return pl.BlockSpec(whole, lambda i, *_: (0, heads[0], 0, 0))

    return call(
        functools.partial(attend_body, blocks, slots, inner),
        (1,),
        [of_heads(HD, BLK), of_heads(HD, BLK), of_heads(2, BLK)]
        + [pl.BlockSpec(memory_space=pl.ANY)] * len(pieces),
        pl.BlockSpec((rows, inner * HD), lambda i, *_: (0, 0)),
        jax.ShapeDtypeStruct((rows, inner * HD), jnp.bfloat16),
        12,
        scratch=[
            pltpu.VMEM((total_blocks, inner, 2, BLK, HD), jnp.bfloat16),
            pltpu.SemaphoreType.DMA((len(pieces),)),
        ],
        prefetch=2,
        micros=ATT_COST,
    )(where_block, counts, queries, past, stats, *pieces)


def part_body(count, state_ref, w_ref, *rest):
    pieces, out_ref = rest[:count], rest[count]
    attended = jnp.concatenate([piece[...] for piece in pieces], axis=1)
    out_ref[...] = (state_ref[...].astype(jnp.float32) + dot(attended, w_ref[...])).astype(out_ref.dtype)


def add_heads(state, w_rows, pieces, out_dtype):
    rows, width = state.shape
    return call(
        functools.partial(part_body, len(pieces)),
        (rows // ADD_TILE,),
        [pl.BlockSpec((ADD_TILE, width), lambda i: (i, 0)), pl.BlockSpec(w_rows.shape, lambda i: (0, 0))]
        + [pl.BlockSpec((ADD_TILE, piece.shape[1]), lambda i: (i, 0)) for piece in pieces],
        pl.BlockSpec((ADD_TILE, width), lambda i: (i, 0)),
        jax.ShapeDtypeStruct((rows, width), out_dtype),
        18,
        micros=PART_COST,
    )(state, w_rows, *pieces)


def turn_body(count, part_ref, w_ref, gain_ref, wk_ref, wv_ref, *rest):
    pieces, (state_ref, kv_ref, facing_ref, kv_scr) = rest[:count], rest[count:]

    @pl.when(pl.program_id(0) == 0)
    def _():
        kv_scr[:, :HD] = wk_ref[...]
        kv_scr[:, HD:] = wv_ref[...]

    attended = jnp.concatenate([piece[...] for piece in pieces], axis=1)
    state = (part_ref[...] + dot(attended, w_ref[...])).astype(jnp.bfloat16)
    state_ref[...] = state
    store_first(kv_ref, facing_ref, dot(normalize(state.astype(jnp.float32), gain_ref[...]), kv_scr[...]))


def turn(part, w_rows, pieces, gain, w_key, w_value):
    rows, width = part.shape
    half = rows // 2
    tile = pl.BlockSpec((half, width), lambda i: (i, 0))
    return call(
        functools.partial(turn_body, len(pieces)),
        (2,),
        [
            tile,
            pl.BlockSpec(w_rows.shape, lambda i: (0, 0)),
            pl.BlockSpec((width,), lambda i: (0,)),
            pl.BlockSpec((width, HD), lambda i: (0, 0)),
            pl.BlockSpec((width, HD), lambda i: (0, 0)),
        ]
        + [pl.BlockSpec((half, piece.shape[1]), lambda i: (i, 0)) for piece in pieces],
        [
            tile,
            pl.BlockSpec((half // BLK, 1, 2, BLK, HD), lambda i: (i, 0, 0, 0, 0)),
            pl.BlockSpec((half // BLK, 1, 2, BLK, HD), lambda i: (0, 0, 0, 0, 0)),
        ],
        [
            jax.ShapeDtypeStruct((rows, width), jnp.bfloat16),
            jax.ShapeDtypeStruct((rows // BLK, 1, 2, BLK, HD), jnp.bfloat16),
            jax.ShapeDtypeStruct((half // BLK, 1, 2, BLK, HD), jnp.bfloat16),
        ],
        18,
        scratch=[pltpu.VMEM((width, 2 * HD), jnp.bfloat16)],
        micros=7.0,
    )(part, w_rows, gain, w_key, w_value, *pieces)


def facing(kv):
    half = kv.shape[0] // 2
    return lax.dynamic_slice_in_dim(kv, half * (1 - lax.axis_index("space") % 2), half, 0)


def halo(kv, faces=None):
    faces = facing(kv) if faces is None else faces
    return sent(kv, across), sent(faces, beyond), sent(kv, beside)


def share_rows(w_out, fetched, then):
    fetched = jnp.stack(fetched)
    count = lax.axis_size("space")
    half = count // 2
    local, width = w_out.shape
    heads = local // HD
    me = lax.axis_index("space")
    second = sent(fetched, beside)
    third = sent(fetched, opposite)
    fourth = sent(after(third, then), beside)
    odd, upper = me % 2 == 1, me >= half
    near = (jnp.where(odd, second, fetched), jnp.where(odd, fetched, second))
    far = (jnp.where(odd, fourth, third), jnp.where(odd, third, fourth))
    four = [jnp.where(upper, b, a) for a, b in zip(near + far, far + near, strict=True)]
    others = jnp.stack(four, axis=2).reshape(-1, heads, HD, width)
    return jnp.concatenate([w_out.reshape(1, heads, HD, width), others])


def on_device(snapshot, norm_gain, w_query, w_key, w_value, w_out, cache_key, cache_value, pattern, counts):
    tok_rows, width = snapshot.shape
    blocks = tok_rows // BLK
    half = blocks // 2
    count = blocks * lax.axis_size("space")
    me = lax.axis_index("space")
    own_block = jnp.arange(blocks, dtype=jnp.int32)[:, None]
    relative = (pattern - own_block - me * blocks + count // 2) % count - count // 2
    place = own_block + blocks + half + relative
    turn_by = jnp.where(place < half + blocks, 2 * blocks, jnp.where(place < half + 2 * blocks, 0, -2 * blocks))
    end = 3 * blocks + half
    turn_by = jnp.where(place < half, end, jnp.where(place >= end, -end, turn_by))
    where_block = jnp.where(me % 2 == 1, place + turn_by, place).reshape(-1)
    state = snapshot
    kv_first, faces, mine = first_projection(state, norm_gain, w_key, w_value, w_out)
    last = []
    for rollout in range(STEPS):
        near = [halo(kv_first, faces)]
        *kv_rest, queries = rest_projection(state, norm_gain, w_query, w_key, w_value, REST_VMEM[rollout])
        kv = [kv_first] + list(kv_rest)
        near += [halo(piece) for piece in kv_rest]
        if rollout == 0:
            fetched = around(mine, "head")[1:]
            queries = after(queries, *fetched[:WPAST])
        past, stats = attend_past(queries, cache_key, cache_value, last)
        came = []
        attended = past
        for chunk, of_chunk in enumerate(CHUNKS):
            next_pair, further, other = near[chunk]
            held = (attended, further) if chunk == 0 and rollout >= C2PIN else (attended,)
            shared = sent(facing(after(next_pair, *held)), beside)
            own = kv[chunk]
            if chunk < 2 and rollout == 0:
                own = after(own, *fetched[: WPINS[chunk]])
            if chunk >= 1:
                own = after(own, *came[-1][1 : ATT_PINS[chunk - 1]])
            pieces = (further, next_pair, own, other, shared)
            attended = attend(of_chunk, where_block, counts, queries, past, stats, pieces)
            if rollout == 0 and chunk == SHARE:
                fetched = [after(piece, attended) for piece in fetched]
            if 1 <= chunk <= SEND_PIN:
                attended = after(attended, *came[-1][SENDALL:])
            came.append(around(attended, "head", came[-1][3:] if came else ()))
        if rollout == 0:
            rows_of = share_rows(w_out, fetched, came[-1][1])
        if rollout == 0:
            w_early = rows_of[:, : CHUNKS[-1][0]].reshape(-1, width)
            w_last = rows_of[:, CHUNKS[-1][0] :].reshape(-1, width)
        early = [piece for group in zip(*came[:-1], strict=True) for piece in group]
        part = add_heads(state, w_early, early, jnp.float32)
        if rollout + 1 < STEPS:
            state, kv_first, faces = turn(part, w_last, came[-1], norm_gain, w_key, w_value)
            last = kv
        else:
            state = add_heads(part, w_last, came[-1], jnp.bfloat16)
    return state


def solution(mesh):
    placed = (
        P("space", None),
        P(),
        P(None, "head"),
        P(None, "head"),
        P(None, "head"),
        P("head", None),
        P(None, "space", "head"),
        P(None, "space", "head"),
        P("space", None),
        P("space"),
    )
    return jax.shard_map(
        on_device, mesh=mesh, in_specs=placed, out_specs=P("space", None), check_vma=False
    )
```
